128 devices in a mesh: seq: 32 (over y, z, core), head: 4 (over x).
Axes of the slice: x: 4, y: 4, z: 4, core: 2. Of those that a mesh axis runs over, the one named last changes fastest.
Arguments:
- qkv: bfloat16 [3, 32768, 768], P(None, ('seq', 'head')), may hold values from -24 to 24
- offsets: int32 [12], P('head'), may hold values from 0 to 63
Outputs:
- attention: bfloat16 [32768, 768], P('seq', 'head')
The draws below stay inside these ranges and needn't reach their ends.
Inputs may be any that keep to these rules, and one draw needn't show every extreme that they name: head h selects, at a level of dilation r, the positions congruent to offsets[h] mod r.
All inputs are finite; a program needn't handle non-finite values.
Results may differ from the reference program's by a relative error of at most 0.0045.
Values may be sent and summed in bfloat16 or wider, within the bound.
A program may use at most 64 MiB of HBM per device.

```python
import jax
import jax.numpy as jnp
from jax import lax

HEADS = 12
HD = 64
D = 768
LEVELS = 4
GROWTH = 4
TOKENS = 32768
SEG = 512


def draw_qkv(key, part):
    key = jax.random.fold_in(key, 11)
    key_list = jax.random.split(key, 1)
    full_shape = (3, TOKENS, D)
    result = jnp.clip(jax.random.normal(key_list[0], full_shape, jnp.float32), -6.0, 6.0)
    return result.astype(jnp.bfloat16)


def with_ends(array, stream_key, least, largest):
    longest = array.shape.index(max(array.shape))
    spots = []
    for shift in (0, 1):
        where = [jax.random.randint(jax.random.fold_in(stream_key, axis), (), 0, length) for axis, length in enumerate(array.shape)]
        where[longest] = (where[longest] + shift) % array.shape[longest]
        spots.append(tuple(where))
    return array.at[spots[0]].set(least).at[spots[1]].set(largest)


def setup_inputs(seed: int = 0) -> dict:
    keys = jax.random.split(jax.random.key(seed), 3)
    return {
        "qkv": draw_qkv(jax.random.fold_in(keys[2], 71), 0),
        "offsets": with_ends(jax.random.randint(keys[1], (HEADS,), 0, GROWTH ** (LEVELS - 1)), jax.random.fold_in(keys[1], 1), 0, (GROWTH ** (LEVELS - 1)) - 1).astype(jnp.int32),
    }


NEG_FILL = -1.0e30


def pick_rows(field_rows, dilation, offsets):
    length, head_count, feat_dim = field_rows.shape
    folded = field_rows.reshape(length // dilation, dilation, head_count, feat_dim)
    chosen = (offsets % dilation).astype(jnp.int32).reshape(1, 1, head_count, 1)
    chosen = jnp.broadcast_to(chosen, (length // dilation, 1, head_count, feat_dim))
    return jnp.take_along_axis(folded, chosen, axis=1)[:, 0]


def spread_rows(values, dilation, offsets, fill_value):
    row_count, head_count = values.shape[0], values.shape[1]
    chosen_mask = jnp.arange(dilation, dtype=jnp.int32)[:, None] == (offsets % dilation).astype(jnp.int32)[None, :]
    extra_dims = values.ndim - 2
    chosen_mask = chosen_mask.reshape((1, dilation, head_count) + (1,) * extra_dims)
    placed = jnp.where(chosen_mask, values[:, None], jnp.asarray(fill_value, values.dtype))
    return placed.reshape((row_count * dilation,) + values.shape[1:])


def attend_block(queries, keys_all, values_all):
    qcount = queries.shape[0]
    block_rows = min(qcount, 512)
    softmax_scale = queries.shape[2] ** -0.5

    def one_block(query_block):
        scores = jnp.einsum("qhe,khe->hqk", query_block.astype(jnp.float32), keys_all.astype(jnp.float32)) * softmax_scale
        top_score = jnp.max(scores, axis=2)
        weights = jnp.exp(scores - top_score[:, :, None])
        denominator = jnp.sum(weights, axis=2)
        rounded = lax.optimization_barrier(weights.astype(jnp.bfloat16))
        numerator = jnp.einsum("hqk,khe->qhe", rounded.astype(jnp.float32), values_all.astype(jnp.float32))
        return numerator, denominator.T, top_score.T

    blocks = queries.reshape((qcount // block_rows, block_rows) + queries.shape[1:])
    numerator, denominator, top_score = lax.map(one_block, blocks)
    head_count = queries.shape[1]
    return (numerator.reshape((qcount,) + queries.shape[1:]), denominator.reshape(qcount, head_count), top_score.reshape(qcount, head_count))


def combine(running, update):
    new_top = jnp.maximum(running[2], update[2])
    old_factor = jnp.exp(running[2] - new_top)
    new_factor = jnp.exp(update[2] - new_top)
    numerator = running[0] * old_factor[:, :, None] + update[0] * new_factor[:, :, None]
    denominator = running[1] * old_factor + update[1] * new_factor
    return numerator, denominator, new_top


def reference(qkv, offsets):
    queries = qkv[0].reshape(TOKENS, HEADS, HD)
    keys_all = qkv[1].reshape(TOKENS, HEADS, HD)
    values_all = qkv[2].reshape(TOKENS, HEADS, HD)
    running = None
    for level_index in range(LEVELS):
        dilation = GROWTH ** level_index
        picked = [pick_rows(field_rows, dilation, offsets) for field_rows in (queries, keys_all, values_all)]
        groups = TOKENS // (dilation * SEG)
        shaped = tuple(field_rows.reshape(groups, SEG, HEADS, HD) for field_rows in picked)

        def per_group(triple):
            return attend_block(triple[0], triple[1], triple[2])

        numerator, denominator, top_score = lax.map(per_group, shaped)
        picked_count = TOKENS // dilation
        update = (spread_rows(numerator.reshape(picked_count, HEADS, HD), dilation, offsets, 0.0),
                  spread_rows(denominator.reshape(picked_count, HEADS), dilation, offsets, 0.0),
                  spread_rows(top_score.reshape(picked_count, HEADS), dilation, offsets, NEG_FILL))
        if level_index == 0:
            running = update
        else:
            running = combine(running, update)
    result = running[0] / running[1][:, :, None]
    return result.reshape(TOKENS, HEADS * HD).astype(jnp.bfloat16)
```

```python
import jax
import jax.numpy as jnp
from jax import lax
from jax.experimental import pallas as pl
from jax.experimental.pallas import tpu as pltpu
from jax.sharding import PartitionSpec as P

HD = 64
GH = 3
NX = 4
NZ = 4
ROWS = 256
MESH = pl.DeviceIdType.MESH
LOW = -1.0e30
BF = jnp.bfloat16
F32 = jnp.float32

L2_STEPS = [(0, dz, dc) for dz in (1, 2, 3) for dc in (0, 1)]
L3_STEPS = [(dy, dz, dc) for dy in (1, 2, 3) for dz in range(NZ) for dc in (0, 1)]


def iota(shape, dim):
    return lax.broadcasted_iota(jnp.int32, shape, dim)


def dot(a, b):
    return jnp.dot(a, b, preferred_element_type=F32)


def dot_t(a, b):
    return lax.dot_general(a, b, (((1,), (1,)), ((), ())), preferred_element_type=F32)


def source_row(i):
    return (i % 4) * 64 + (i // 4 % 4) * 16 + (i // 16 % 4) * 4 + i // 64


def digits_of(o):
    return o & 3, (o >> 2) & 3, (o >> 4) & 3


def bits(o, shape):
    spread_out = jnp.zeros(shape, jnp.int32) + o
    return [(spread_out >> i) & 1 == 1 for i in range(4)]


def turn(parts, mask, step):
    return [jnp.where(mask, parts[(i + step) % len(parts)], part) for i, part in enumerate(parts)]


def pick(four, low_bit, high_bit):
    return jnp.where(high_bit, jnp.where(low_bit, four[3], four[2]), jnp.where(low_bit, four[1], four[0]))


def lanes_low(shape):
    return iota(shape, 1) < HD


def soften(scores):
    top = jnp.max(scores, axis=1, keepdims=True)
    return jnp.exp(scores - top).astype(BF), top


def ones_and_values(kv):
    return jnp.where(lanes_low(kv.shape), jnp.ones_like(kv), kv)


def merge(a, a_top, b, b_top):
    top = jnp.maximum(a_top, b_top)
    return a * jnp.exp(a_top - top) + b * jnp.exp(b_top - top), top


def spread(part, w):
    pieces = []
    for j in range(NX):
        pieces += [part[j * w : (j + 1) * w]] * 4
    return jnp.concatenate(pieces, axis=0)


def kernel(
    qkv, offs, out,
    xin, perm, qs, kvs, kvrel, qr, qz, kv, k1s, q2s, k2, k3own, k3, sm, n0, t0, n1, t1, outp,
    in_sem, own_sem, o_send, o_recv, q_send, q_recv, s_send, s_recv, r_send, r_recv,
    c_send, c_recv, l2_send, l2_recv, l3_send, l3_recv,
):
    s = lax.axis_index("seq")
    x = lax.axis_index("head")
    core, z, y = s % 2, s // 2 % NZ, s // (2 * NZ)

    def along_x(k):
        return (s, (x + k) % NX)

    def along_seq(step):
        dy, dz, dc = step
        return ((y + dy) % 4 * (2 * NZ) + (z + dz) % NZ * 2 + (core + dc) % 2, x)

    sibling = along_seq((0, 0, 1))
    barrier = pltpu.get_barrier_semaphore()
    peers = [along_x(k) for k in (1, 2, 3)] + [sibling] + [along_seq(t) for t in L2_STEPS + L3_STEPS]
    for peer in peers:
        pl.semaphore_signal(barrier, inc=1, device_id=peer, device_id_type=MESH)

    loads = [pltpu.make_async_copy(qkv.at[i], xin.at[i], in_sem.at[i]) for i in range(3)]
    for load in loads:
        load.start()

    def remote(src, dst, send, recv, peer):
        return pltpu.make_async_remote_copy(
            src_ref=src, dst_ref=dst, send_sem=send, recv_sem=recv, device_id=peer, device_id_type=MESH
        )

    a, b = iota((ROWS, ROWS), 0), iota((ROWS, ROWS), 1)
    forth = jnp.where(b == source_row(a), 1.0, 0.0).astype(BF)
    perm[...] = jnp.where(a == source_row(b), 1.0, 0.0).astype(BF)
    low = lanes_low((ROWS, 128))
    low_half = lanes_low((128, 128))

    for i in range(GH):
        sm[x, i] = offs[i]

    loads[0].wait()
    forth_scaled = forth * jnp.asarray(HD**-0.5, BF)
    for t in range(3):
        wide = dot(forth_scaled, xin[0, :, t * 256 : (t + 1) * 256])
        for u in range(4):
            head = 4 * t + u
            tile = wide[:, u // 2 * 128 : (u // 2 + 1) * 128]
            first, second = tile[:128], tile[128:]
            if u % 2 == 0:
                packed = jnp.where(low_half, first, pltpu.roll(second, HD, 1))
            else:
                packed = jnp.where(low_half, pltpu.roll(first, HD, 1), second)
            qs[head // GH, head % GH] = packed.astype(BF)

    pl.semaphore_wait(barrier, len(peers))
    sends = []

    def send(*args):
        copy = remote(*args)
        copy.start()
        sends.append(copy)
        return copy

    o_copies = [send(sm.at[x], sm.at[x], o_send.at[k - 1], o_recv.at[k - 1], along_x(k)) for k in (1, 2, 3)]
    q_copies = [
        [
            send(qs.at[(x + k) % NX, hh], qr.at[hh, x], q_send.at[hh, k - 1], q_recv.at[hh, k - 1], along_x(k))
            for k in (1, 3, 2)
        ]
        for hh in range(GH)
    ]
    own_q = pltpu.make_async_copy(qs.at[x], qr.at[:, x], own_sem.at[0])
    own_q.start()

    loads[1].wait()
    loads[2].wait()
    for t in range(6):
        both = jnp.concatenate(
            [xin[1, :, t * 128 : (t + 1) * 128], xin[2, :, t * 128 : (t + 1) * 128]], axis=1
        )
        wide = dot(forth, both)
        keys, values = wide[:, :128], wide[:, 128:]
        even = jnp.where(low, keys, pltpu.roll(values, HD, 1))
        odd = jnp.where(low, pltpu.roll(keys, HD, 1), values)
        for head, packed in ((2 * t, even), (2 * t + 1, odd)):
            kvs[head // GH, head % GH] = packed.astype(BF)

    for copy in o_copies:
        copy.wait_recv()
    for g in range(NX):
        for hh in range(GH):
            b0, b1, b2, b3 = bits(sm[g, hh], (16, 128))
            parts = [kvs[g, hh, i * 16 : (i + 1) * 16, :] for i in range(16)]
            parts = turn(turn(parts, b0, 4), b1, 8)
            parts[:4] = turn(turn(parts[:4], b2, 1), b3, 2)
            for i in range(16):
                kvrel[g, hh, i * 16 : (i + 1) * 16, :] = parts[i]
    s_copies = [
        send(
            kvrel.at[(x + k) % NX, :, pl.ds(0, 64), :], kv.at[:, x, pl.ds(0, 64), :],
            s_send.at[k - 1], s_recv.at[k - 1], along_x(k),
        )
        for k in (1, 3, 2)
    ]
    r_copies = [
        [
            send(
                kvrel.at[(x + k) % NX, hh, pl.ds(64, 192), :], kv.at[hh, x, pl.ds(64, 192), :],
                r_send.at[hh, k - 1], r_recv.at[hh, k - 1], along_x(k),
            )
            for k in (1, 3, 2)
        ]
        for hh in range(GH)
    ]
    own_kv = pltpu.make_async_copy(kvrel.at[x], kv.at[:, x], own_sem.at[1])
    own_kv.start()

    digits = []
    for hh in range(GH):
        o = sm[x, hh]
        digits.append(digits_of(o))

    own_q.wait()
    for hh in range(GH):
        for copy in q_copies[hh]:
            copy.wait_recv()
        for j in range(NX):
            tile = qr[hh, j].astype(F32)
            qz[hh, j, 0:128, :] = jnp.where(low_half, tile, 0.0).astype(BF)
            qz[hh, j, 128:256, :] = jnp.where(low_half, pltpu.roll(tile, HD, 1), 0.0).astype(BF)

    own_kv.wait()
    for copy in s_copies:
        copy.wait_recv()
    c_copy = send(kv.at[:, :, pl.ds(0, 64), :], k1s, c_send, c_recv, sibling)
    l2_copies = [
        send(kv.at[:, :, pl.ds(0, 16), :], k2.at[i], l2_send.at[i], l2_recv.at[i], along_seq(step))
        for i, step in enumerate(L2_STEPS)
    ]
    e_row, e_col = iota((16, 64), 0), iota((16, 64), 1)
    for hh in range(GH):
        chosen = jnp.where(e_col == e_row // 4 * 16 + digits[hh][2] * 4 + e_row % 4, 1.0, 0.0).astype(BF)
        k3own[hh] = dot(chosen, kv[hh, :, 0:16, :].reshape(64, 128)).astype(BF)
    l3_copies = [
        send(k3own, k3.at[i], l3_send.at[i], l3_recv.at[i], along_seq(step)) for i, step in enumerate(L3_STEPS)
    ]

    c_copy.wait_recv()
    for hh in range(GH):
        b0, b1, b2, b3 = bits(sm[x, hh], (16, 128))
        q1 = []
        for j in range(NX):
            parts = [qz[hh, j, i * 16 : (i + 1) * 16, :] for i in range(16)]
            chosen = [pick(parts[i::4], b0, b1) for i in range(4)]
            q1 += chosen
            q2s[hh, j] = pick(chosen, b2, b3)
        q1 = jnp.concatenate(q1, axis=0)
        keys = jnp.concatenate([kv[hh, :, 0:64, :].reshape(256, 128), k1s[hh].reshape(256, 128)], axis=0)
        weights, top = soften(dot_t(q1, keys))
        n1[hh] = dot(weights, ones_and_values(keys))
        t1[hh] = top

    for hh in range(GH):
        for copy in r_copies[hh]:
            copy.wait_recv()
        for seg in range(2):
            keys = kv[hh, 2 * seg : 2 * seg + 2].reshape(512, 128)
            values = ones_and_values(keys)
            for j in (2 * seg, 2 * seg + 1):
                weights, top = soften(dot_t(qz[hh, j], keys))
                n0[hh, j] = dot(weights, values)
                t0[hh, j] = top

    for copy in l2_copies + l3_copies:
        copy.wait_recv()
    col = iota((64, 512), 1)
    for hh in range(GH):
        c1, c2, c3 = digits[hh]
        q2 = q2s[hh].reshape(64, 128)
        keys2 = jnp.concatenate(
            [kv[hh, :, 0:16, :].reshape(64, 128), k1s[hh, :, 0:16, :].reshape(64, 128)]
            + [k2[i, hh].reshape(64, 128) for i in range(len(L2_STEPS))],
            axis=0,
        )
        keys3 = jnp.concatenate([k3[i, hh] for i in range(len(L3_STEPS))], axis=0)
        scores2 = dot_t(q2, keys2)
        scores3 = jnp.concatenate(
            [jnp.where(col % 16 // 4 == c3, scores2, LOW), dot_t(q2, keys3)], axis=1
        )
        weights2, top2 = soften(scores2)
        weights3, top3 = soften(scores3)
        values2 = ones_and_values(keys2)
        num2 = dot(weights2, values2)
        num3 = dot(weights3[:, :512], values2) + dot(weights3[:, 512:], ones_and_values(keys3))
        row = iota((64, 1), 0)
        num2, top2 = merge(num2, top2, num3, jnp.where(row % 16 // 4 == c3, top3, LOW))

        row = iota((ROWS, 1), 0)
        num1, top1 = merge(
            n1[hh], t1[hh], spread(num2, 16), jnp.where(row % 64 // 16 == c2, spread(top2, 16), LOW)
        )

        b0, b1, _, _ = bits(sm[x, hh], (64, 128))
        part = jnp.concatenate(
            [pick([n0[hh, j, i * 64 : (i + 1) * 64, :] for i in range(4)], b0, b1) for j in range(NX)], axis=0
        )
        b0, b1, _, _ = bits(sm[x, hh], (64, 1))
        part_top = jnp.concatenate(
            [pick([t0[hh, j, i * 64 : (i + 1) * 64, :] for i in range(4)], b0, b1) for j in range(NX)], axis=0
        )
        num0, _ = merge(part, part_top, num1, top1)
        low64 = lanes_low((64, 128))
        for j in range(NX):
            merged = num0[j * 64 : (j + 1) * 64]
            whole = n0[hh, j]
            mine = iota((ROWS, 1), 0) // 64 == c1
            whole = jnp.where(mine, jnp.concatenate([merged] * 4, axis=0), whole)
            turned = pltpu.roll(whole, HD, 1)
            if hh % 2 == 0:
                value = (turned / whole).astype(BF)
                outp[j, :, hh // 2 * 128 : (hh // 2 + 1) * 128] = value
            else:
                value = (whole / turned).astype(BF)
                outp[j, :, 0:128] = jnp.where(low, outp[j, :, 0:128], value)
    for j in range(NX):
        final = dot(perm[...], outp[j])
        out[j * ROWS : (j + 1) * ROWS, :] = final[:, : GH * HD].astype(BF)

    for copy in sends:
        copy.wait_send()


def per_device(qkv, offsets):
    dma = pltpu.SemaphoreType.DMA
    return pl.pallas_call(
        kernel,
        out_shape=jax.ShapeDtypeStruct((NX * ROWS, GH * HD), BF),
        in_specs=[pl.BlockSpec(memory_space=pl.ANY), pl.BlockSpec(memory_space=pltpu.SMEM)],
        out_specs=pl.BlockSpec(memory_space=pltpu.VMEM),
        scratch_shapes=[
            pltpu.VMEM((3, ROWS, 768), BF),
            pltpu.VMEM((ROWS, ROWS), BF),
            pltpu.VMEM((NX, GH, 128, 128), BF),
            pltpu.VMEM((NX, GH, ROWS, 128), BF),
            pltpu.VMEM((NX, GH, ROWS, 128), BF),
            pltpu.VMEM((GH, NX, 128, 128), BF),
            pltpu.VMEM((GH, NX, ROWS, 128), BF),
            pltpu.VMEM((GH, NX, ROWS, 128), BF),
            pltpu.VMEM((GH, NX, 64, 128), BF),
            pltpu.VMEM((GH, NX, 16, 128), BF),
            pltpu.VMEM((len(L2_STEPS), GH, NX, 16, 128), BF),
            pltpu.VMEM((GH, 16, 128), BF),
            pltpu.VMEM((len(L3_STEPS), GH, 16, 128), BF),
            pltpu.SMEM((NX, 128), jnp.int32),
            pltpu.VMEM((GH, NX, ROWS, 128), F32),
            pltpu.VMEM((GH, NX, ROWS, 1), F32),
            pltpu.VMEM((GH, ROWS, 128), F32),
            pltpu.VMEM((GH, ROWS, 1), F32),
            pltpu.VMEM((NX, ROWS, 256), BF),
            dma((3,)), dma((2,)), dma((3,)), dma((3,)),
            dma((GH, 3)), dma((GH, 3)), dma((3,)), dma((3,)), dma((GH, 3)), dma((GH, 3)),
            dma, dma, dma((len(L2_STEPS),)), dma((len(L2_STEPS),)), dma((len(L3_STEPS),)), dma((len(L3_STEPS),)),
        ],
        compiler_params=pltpu.CompilerParams(
            collective_id=0, has_side_effects=True, vmem_limit_bytes=40 * 2**20
        ),
        cost_estimate=pl.CostEstimate(flops=10**9, bytes_accessed=2 * 10**6, transcendentals=2 * 10**6),
    )(qkv, offsets)


def solution(mesh):
    return jax.shard_map(
        per_device,
        mesh=mesh,
        in_specs=(P(None, ("seq", "head"), None), P("head")),
        out_specs=P("seq", "head"),
        check_vma=False,
    )
```

```python
import jax
import jax.numpy as jnp
from jax import lax
from jax.experimental import pallas as pl
from jax.experimental.pallas import tpu as pltpu
from jax.sharding import PartitionSpec as P

HD = 64
GH = 3
NX = 4
NY = 4
NZ = 4
ROWS = 256
MESH = pl.DeviceIdType.MESH
LOW = -1.0e30
BF = jnp.bfloat16
F32 = jnp.float32

L2_STEPS = [(0, dz) for dz in (2, 1, 3)]
L3_STEPS = [(dy, dz) for dy in (2, 1, 3) for dz in (2, 1, 3, 0)]
N2, N3 = len(L2_STEPS), len(L3_STEPS)


def iota(shape, dim):
    return lax.broadcasted_iota(jnp.int32, shape, dim)


def dot(a, b):
    return jnp.dot(a, b, preferred_element_type=F32)


def dot_t(a, b):
    return lax.dot_general(a, b, (((1,), (1,)), ((), ())), preferred_element_type=F32)


def source_row(i):
    return (i % 4) * 64 + (i // 4 % 4) * 16 + (i // 16 % 4) * 4 + i // 64


def bits(o, shape):
    spread_out = jnp.zeros(shape, jnp.int32) + o
    return [(spread_out >> i) & 1 == 1 for i in range(4)]


def turn(parts, mask, step):
    return [jnp.where(mask, parts[(i + step) % len(parts)], part) for i, part in enumerate(parts)]


def pick(four, low_bit, high_bit):
    return jnp.where(high_bit, jnp.where(low_bit, four[3], four[2]), jnp.where(low_bit, four[1], four[0]))


def lanes_low(shape):
    return iota(shape, 1) < HD


def soften(scores):
    top = jnp.max(scores, axis=1, keepdims=True)
    return jnp.exp(scores - top).astype(BF), top


def ones_and_values(kv):
    return jnp.where(lanes_low(kv.shape), jnp.ones_like(kv), kv)


def merge(a, a_top, b, b_top):
    top = jnp.maximum(a_top, b_top)
    return a * jnp.exp(a_top - top) + b * jnp.exp(b_top - top), top


def spread(part, w):
    pieces = []
    for j in range(NX):
        pieces += [part[j * w : (j + 1) * w]] * 4
    return jnp.concatenate(pieces, axis=0)


def quotient(num, low_side):
    turned = pltpu.roll(num, HD, 1)
    return turned / num if low_side else num / turned


def order_of(y, z):
    return (8 * z + 7 * jnp.minimum(y, 2) + y // 3) * 4 + y


def kernel(
    qkv, offs, out,
    xin, perm, qs, kvs, kvrel, qr, qz, kv, k1s, q2s, k2, k3own, k3, osm, sm, n0, t0, n1, t1, outp,
    in_sem, own_sem, o_send, o_recv, q_send, q_recv, s_send, s_recv, u_send, u_recv, r_send, r_recv,
    c_send, c_recv, l2_send, l2_recv, l3_send, l3_recv, f_send, f_recv, ready,
):
    s = lax.axis_index("seq")
    x = lax.axis_index("head")
    core, z, y = s % 2, s // 2 % NZ, s // (2 * NZ)

    def along_x(k):
        return (s, (x + k) % NX)

    def along_seq(step):
        return ((y + step[0]) % NY * (2 * NZ) + (z + step[1]) % NZ * 2 + core, x)

    mine = order_of(y, z)

    def later(step):
        return order_of((y + step[0]) % NY, (z + step[1]) % NZ) > mine

    sibling = (s + 1 - 2 * core, x)
    barrier = pltpu.get_barrier_semaphore()
    near = [along_x(k) for k in (1, 2, 3)] + [sibling]
    for peer in near:
        pl.semaphore_signal(barrier, inc=1, device_id=peer, device_id_type=MESH)

    for step in L2_STEPS + L3_STEPS:

        @pl.when(later(step))
        def _():
            pl.semaphore_signal(barrier, inc=1, device_id=along_seq(step), device_id_type=MESH)

    own_offs = pltpu.make_async_copy(offs, osm, own_sem.at[2])
    own_offs.start()
    loads = [pltpu.make_async_copy(qkv.at[i], xin.at[i], in_sem.at[i]) for i in range(3)]
    for load in loads:
        load.start()

    n_later = jnp.int32(0)
    for step in L2_STEPS + L3_STEPS:
        n_later = n_later + jnp.where(later(step), 1, 0)
    n_earlier = len(L2_STEPS + L3_STEPS) - n_later

    sends = []

    def send(src, dst, send_sem, recv_sem, peer):
        copy = pltpu.make_async_remote_copy(
            src_ref=src, dst_ref=dst, send_sem=send_sem, recv_sem=recv_sem, device_id=peer, device_id_type=MESH
        )
        copy.start()
        sends.append(copy)
        return copy

    a, b = iota((ROWS, ROWS), 0), iota((ROWS, ROWS), 1)
    forth = jnp.where(b == source_row(a), 1.0, 0.0).astype(BF)
    perm[...] = forth
    low = lanes_low((ROWS, 128))
    low_half = lanes_low((128, 128))

    loads[0].wait()
    forth_scaled = forth * jnp.asarray(HD**-0.5, BF)
    for t in range(3):
        wide = dot(forth_scaled, xin[0, :, t * 256 : (t + 1) * 256])
        for u in range(4):
            head = 4 * t + u
            tile = wide[:, u // 2 * 128 : (u // 2 + 1) * 128]
            first, second = tile[:128], tile[128:]
            if u % 2 == 0:
                packed = jnp.where(low_half, first, pltpu.roll(second, HD, 1))
            else:
                packed = jnp.where(low_half, pltpu.roll(first, HD, 1), second)
            qs[head // GH, head % GH] = packed.astype(BF)

    own_offs.wait()
    for i in range(GH):
        sm[x, i] = osm[i]

    pl.semaphore_wait(barrier, len(near) + n_earlier)

    o_copies = [send(sm.at[x], sm.at[x], o_send.at[k - 1], o_recv.at[k - 1], along_x(k)) for k in (1, 2, 3)]

    def send_q(hh):
        return [
            send(qs.at[(x + k) % NX, hh], qr.at[hh, x], q_send.at[hh, k - 1], q_recv.at[hh, k - 1], along_x(k))
            for k in (1, 3, 2)
        ]

    q_copies = [send_q(0), send_q(1)]
    for step in L2_STEPS + L3_STEPS:

        @pl.when(jnp.logical_not(later(step)))
        def _():
            pl.semaphore_signal(ready, inc=1, device_id=along_seq(step), device_id_type=MESH)

    own_q = pltpu.make_async_copy(qs.at[x], qr.at[:, x], own_sem.at[0])
    own_q.start()

    loads[1].wait()
    loads[2].wait()
    for t in range(6):
        both = jnp.concatenate(
            [xin[1, :, t * 128 : (t + 1) * 128], xin[2, :, t * 128 : (t + 1) * 128]], axis=1
        )
        wide = dot(forth, both)
        keys, values = wide[:, :128], wide[:, 128:]
        even = jnp.where(low, keys, pltpu.roll(values, HD, 1))
        odd = jnp.where(low, pltpu.roll(keys, HD, 1), values)
        for head, packed in ((2 * t, even), (2 * t + 1, odd)):
            kvs[head // GH, head % GH] = packed.astype(BF)

    for copy in o_copies:
        copy.wait_recv()

    def send_rows(first, count, send_sem, recv_sem):
        own = pltpu.make_async_copy(
            kvrel.at[x, :, pl.ds(first, count), :], kv.at[:, x, pl.ds(first, count), :], own_sem.at[3 + first // 16]
        )
        own.start()
        return own, [
            send(
                kvrel.at[(x + k) % NX, :, pl.ds(first, count), :], kv.at[:, x, pl.ds(first, count), :],
                send_sem.at[k - 1], recv_sem.at[k - 1], along_x(k),
            )
            for k in (1, 3, 2)
        ]

    for g in range(NX):
        for hh in range(GH):
            b0, b1, b2, b3 = bits(sm[g, hh], (16, 128))
            parts = [kvs[g, hh, i * 16 : (i + 1) * 16, :] for i in range(16)]
            kvrel[g, hh, 0:16, :] = pick([pick(parts[i::4], b0, b1) for i in range(4)], b2, b3)
    own_s, s_copies = send_rows(0, 16, s_send, s_recv)
    for g in range(NX):
        for hh in range(GH):
            b0, b1, b2, b3 = bits(sm[g, hh], (16, 128))
            parts = [kvs[g, hh, i * 16 : (i + 1) * 16, :] for i in range(16)]
            parts = turn(turn(parts, b0, 4), b1, 8)
            parts[:4] = turn(turn(parts[:4], b2, 1), b3, 2)
            for i in range(1, 16):
                kvrel[g, hh, i * 16 : (i + 1) * 16, :] = parts[i]
    own_u, u_copies = send_rows(16, 48, u_send, u_recv)
    q_copies.append(send_q(2))
    r_copies = [
        [
            send(
                kvrel.at[(x + k) % NX, hh, pl.ds(64, 192), :], kv.at[hh, x, pl.ds(64, 192), :],
                r_send.at[hh, k - 1], r_recv.at[hh, k - 1], along_x(k),
            )
            for k in (1, 3, 2)
        ]
        for hh in range(GH)
    ]
    own_r = pltpu.make_async_copy(kvrel.at[x, :, pl.ds(64, 192), :], kv.at[:, x, pl.ds(64, 192), :], own_sem.at[1])
    own_r.start()

    digits = []
    for hh in range(GH):
        o = sm[x, hh]
        digits.append((o & 3, (o >> 2) & 3, (o >> 4) & 3))

    own_s.wait()
    for copy in s_copies:
        copy.wait_recv()
    e_row, e_col = iota((16, 64), 0), iota((16, 64), 1)
    for hh in range(GH):
        chosen = jnp.where(e_col == e_row // 4 * 16 + digits[hh][2] * 4 + e_row % 4, 1.0, 0.0).astype(BF)
        k3own[hh] = dot(chosen, kv[hh, :, 0:16, :].reshape(64, 128)).astype(BF)

    @pl.when(n_later > 0)
    def _():
        pl.semaphore_wait(ready, n_later)

    l3_copies = [
        send(k3own, k3.at[i], l3_send.at[i], l3_recv.at[i], along_seq(step)) for i, step in enumerate(L3_STEPS)
    ]
    l2_copies = [
        send(kv.at[:, :, pl.ds(0, 16), :], k2.at[i], l2_send.at[i], l2_recv.at[i], along_seq(step))
        for i, step in enumerate(L2_STEPS)
    ]
    own_u.wait()
    for copy in u_copies:
        copy.wait_recv()
    c_copy = send(kv.at[:, :, pl.ds(0, 64), :], k1s, c_send, c_recv, sibling)

    own_q.wait()
    for hh in range(GH):
        for copy in q_copies[hh]:
            copy.wait_recv()
        for j in range(NX):
            tile = qr[hh, j].astype(F32)
            qz[hh, j, 0:128, :] = jnp.where(low_half, tile, 0.0).astype(BF)
            qz[hh, j, 128:256, :] = jnp.where(low_half, pltpu.roll(tile, HD, 1), 0.0).astype(BF)

    c_copy.wait_recv()
    for hh in range(GH):
        b0, b1, b2, b3 = bits(sm[x, hh], (16, 128))
        q1 = []
        for j in range(NX):
            parts = [qz[hh, j, i * 16 : (i + 1) * 16, :] for i in range(16)]
            chosen = [pick(parts[i::4], b0, b1) for i in range(4)]
            q1 += chosen
            q2s[hh, j] = pick(chosen, b2, b3)
        q1 = jnp.concatenate(q1, axis=0)
        keys = jnp.concatenate([kv[hh, :, 0:64, :].reshape(256, 128), k1s[hh].reshape(256, 128)], axis=0)
        weights, top = soften(dot_t(q1, keys))
        n1[hh] = dot(weights, ones_and_values(keys))
        t1[hh] = top

    own_r.wait()
    for hh in range(GH):
        for copy in r_copies[hh]:
            copy.wait_recv()
        for seg in range(2):
            keys = kv[hh, 2 * seg : 2 * seg + 2].reshape(512, 128)
            values = ones_and_values(keys)
            for j in (2 * seg, 2 * seg + 1):
                weights, top = soften(dot_t(qz[hh, j], keys))
                num = dot(weights, values)
                n0[hh, j] = num
                t0[hh, j] = top
                value = quotient(num, hh % 2 == 0).astype(BF)
                if hh % 2 == 1:
                    value = jnp.where(low, outp[j, :, 0:128], value)
                outp[j, :, hh // 2 * 128 : (hh // 2 + 1) * 128] = value
        if hh == 0:
            for copy in l2_copies:
                copy.wait_recv()
            f2_copy = send(k2.at[pl.ds(0, N2)], k2.at[pl.ds(N2, N2)], f_send.at[0], f_recv.at[0], sibling)
        if hh == 1:
            for copy in l3_copies:
                copy.wait_recv()
            f3_copy = send(k3.at[pl.ds(0, N3)], k3.at[pl.ds(N3, N3)], f_send.at[1], f_recv.at[1], sibling)

    f2_copy.wait_recv()
    f3_copy.wait_recv()
    col = iota((64, 512), 1)
    row64 = iota((64, 1), 0)
    row256 = iota((ROWS, 1), 0)
    low16 = lanes_low((16, 128))
    for hh in range(GH):
        c1, c2, c3 = digits[hh]
        q2 = q2s[hh].reshape(64, 128)
        keys2 = jnp.concatenate(
            [kv[hh, :, 0:16, :].reshape(64, 128), k1s[hh, :, 0:16, :].reshape(64, 128)]
            + [k2[i, hh].reshape(64, 128) for i in range(2 * N2)],
            axis=0,
        )
        keys3 = jnp.concatenate([k3[i, hh] for i in range(2 * N3)], axis=0)
        values2 = ones_and_values(keys2)
        scores2 = dot_t(q2, keys2)
        weights2, top2 = soften(scores2)
        weights3, top3 = soften(
            jnp.concatenate([jnp.where(col % 16 // 4 == c3, scores2, LOW), dot_t(q2, keys3)], axis=1)
        )
        num3 = dot(weights3[:, :512], values2) + dot(weights3[:, 512:], ones_and_values(keys3))
        num2, top2 = merge(
            dot(weights2, values2), top2, num3, jnp.where(row64 % 16 // 4 == c3, top3, LOW)
        )
        num1, top1 = merge(
            n1[hh], t1[hh], spread(num2, 16), jnp.where(row256 % 64 // 16 == c2, spread(top2, 16), LOW)
        )
        b0, b1, _, _ = bits(sm[x, hh], (64, 128))
        part = jnp.concatenate(
            [pick([n0[hh, j, i * 64 : (i + 1) * 64, :] for i in range(4)], b0, b1) for j in range(NX)], axis=0
        )
        b0, b1, _, _ = bits(sm[x, hh], (64, 1))
        part_top = jnp.concatenate(
            [pick([t0[hh, j, i * 64 : (i + 1) * 64, :] for i in range(4)], b0, b1) for j in range(NX)], axis=0
        )
        num, _ = merge(part, part_top, num1, top1)
        value = quotient(num, hh % 2 == 0).astype(BF)
        place = jnp.zeros((16, 128), jnp.int32) + c1
        side = [low16, jnp.logical_not(low16), low16][hh]
        masks = [(place == i) & side for i in range(4)]
        lanes = slice(hh // 2 * 128, (hh // 2 + 1) * 128)
        for j in range(NX):
            for i in range(16):
                new = value[j * 64 + i % 4 * 16 : j * 64 + i % 4 * 16 + 16]
                rows = slice(i * 16, (i + 1) * 16)
                outp[j, rows, lanes] = jnp.where(masks[i // 4], new, outp[j, rows, lanes])
    for j in range(NX):
        final = lax.dot_general(
            outp[j], perm[...], (((0,), (0,)), ((), ())), preferred_element_type=F32
        )
        out[:, j * ROWS : (j + 1) * ROWS] = final[: GH * HD].astype(BF)

    for copy in sends:
        copy.wait_send()


def per_device(qkv, offsets):
    dma = pltpu.SemaphoreType.DMA
    turned = pl.pallas_call(
        kernel,
        out_shape=jax.ShapeDtypeStruct((GH * HD, NX * ROWS), BF),
        in_specs=[pl.BlockSpec(memory_space=pltpu.HBM), pl.BlockSpec(memory_space=pltpu.HBM)],
        out_specs=pl.BlockSpec(memory_space=pltpu.VMEM),
        scratch_shapes=[
            pltpu.VMEM((3, ROWS, 768), BF),
            pltpu.VMEM((ROWS, ROWS), BF),
            pltpu.VMEM((NX, GH, 128, 128), BF),
            pltpu.VMEM((NX, GH, ROWS, 128), BF),
            pltpu.VMEM((NX, GH, ROWS, 128), BF),
            pltpu.VMEM((GH, NX, 128, 128), BF),
            pltpu.VMEM((GH, NX, ROWS, 128), BF),
            pltpu.VMEM((GH, NX, ROWS, 128), BF),
            pltpu.VMEM((GH, NX, 64, 128), BF),
            pltpu.VMEM((GH, NX, 16, 128), BF),
            pltpu.VMEM((2 * N2, GH, NX, 16, 128), BF),
            pltpu.VMEM((GH, 16, 128), BF),
            pltpu.VMEM((2 * N3, GH, 16, 128), BF),
            pltpu.SMEM((GH,), jnp.int32),
            pltpu.SMEM((NX, 128), jnp.int32),
            pltpu.VMEM((GH, NX, ROWS, 128), F32),
            pltpu.VMEM((GH, NX, ROWS, 1), F32),
            pltpu.VMEM((GH, ROWS, 128), F32),
            pltpu.VMEM((GH, ROWS, 1), F32),
            pltpu.VMEM((NX, ROWS, 256), BF),
            dma((3,)), dma((5,)), dma((3,)), dma((3,)), dma((GH, 3)), dma((GH, 3)), dma((3,)), dma((3,)),
            dma((3,)), dma((3,)), dma((GH, 3)), dma((GH, 3)), dma, dma, dma((N2,)), dma((N2,)), dma((N3,)), dma((N3,)),
            dma((2,)), dma((2,)),
            pltpu.SemaphoreType.REGULAR,
        ],
        compiler_params=pltpu.CompilerParams(
            collective_id=0, has_side_effects=True, vmem_limit_bytes=40 * 2**20
        ),
        cost_estimate=pl.CostEstimate(flops=10**9, bytes_accessed=2 * 10**6, transcendentals=2 * 10**6),
    )(qkv, offsets)
    return turned.T


def solution(mesh):
    return jax.shard_map(
        per_device,
        mesh=mesh,
        in_specs=(P(None, ("seq", "head"), None), P("head")),
        out_specs=P("seq", "head"),
        check_vma=False,
    )
```

```python
import jax
import jax.numpy as jnp
from jax import lax
from jax.experimental import pallas as pl
from jax.experimental.pallas import tpu as pltpu
from jax.sharding import PartitionSpec as P

HD = 64
GH = 3
NX = 4
NY = 4
NZ = 4
ROWS = 256
MESH = pl.DeviceIdType.MESH
LOW = -1.0e30
BF = jnp.bfloat16
F32 = jnp.float32

L2_STEPS = [(0, dz) for dz in (2, 1, 3)]
L3_STEPS = [(dy, dz) for dy in (2, 1, 3) for dz in (2, 1, 3, 0)]
N2, N3 = len(L2_STEPS), len(L3_STEPS)


def iota(shape, dim):
    return lax.broadcasted_iota(jnp.int32, shape, dim)


def dot(a, b):
    return jnp.dot(a, b, preferred_element_type=F32)


def dot_t(a, b):
    return lax.dot_general(a, b, (((1,), (1,)), ((), ())), preferred_element_type=F32)


def source_row(i):
    return ((i & 3) << 6) | ((i & 12) << 2) | ((i & 48) >> 2) | (i >> 6)


def bits(o, shape):
    spread_out = jnp.zeros(shape, jnp.int32) + o
    return [(spread_out >> i) & 1 == 1 for i in range(4)]


def turn(parts, mask, step):
    return [jnp.where(mask, parts[(i + step) % len(parts)], part) for i, part in enumerate(parts)]


def pick(four, low_bit, high_bit):
    return jnp.where(high_bit, jnp.where(low_bit, four[3], four[2]), jnp.where(low_bit, four[1], four[0]))


def lanes_low(shape):
    return iota(shape, 1) < HD


def soften(scores):
    top = jnp.max(scores, axis=1, keepdims=True)
    return jnp.exp(scores - top).astype(BF), top


def ones_and_values(kv):
    return jnp.where(lanes_low(kv.shape), jnp.ones_like(kv), kv)


def merge(a, a_top, b, b_top):
    top = jnp.maximum(a_top, b_top)
    return a * jnp.exp(a_top - top) + b * jnp.exp(b_top - top), top


def spread(part, w):
    pieces = []
    for j in range(NX):
        pieces += [part[j * w : (j + 1) * w]] * 4
    return jnp.concatenate(pieces, axis=0)


def quotient(num, low_side):
    turned = pltpu.roll(num, HD, 1)
    return turned / num if low_side else num / turned


def order_of(y, z):
    return (8 * z + 7 * jnp.minimum(y, 2) + jnp.where(y == 3, 1, 0)) * 4 + y


def kernel(
    qkv, offs, out,
    xin, perm, qs, kvs, kvrel, qr, qz, kv, k1s, q2s, k2, k3own, k3, osm, sm, n0, t0, n1, t1, s2, v2, n2, t2, outp,
    in_sem, own_sem, o_send, o_recv, q_send, q_recv, s_send, s_recv, u_send, u_recv, r_send, r_recv,
    c_send, c_recv, l2_send, l2_recv, l3_send, l3_recv, f_send, f_recv, ready,
):
    s = lax.axis_index("seq")
    x = lax.axis_index("head")
    core, z, y = lax.rem(s, 2), lax.rem(lax.div(s, 2), NZ), lax.div(s, 2 * NZ)

    def along_x(k):
        return (s, lax.rem(x + k, NX))

    def along_seq(step):
        return (lax.rem(y + step[0], NY) * (2 * NZ) + lax.rem(z + step[1], NZ) * 2 + core, x)

    mine = order_of(y, z)

    def later(step):
        return order_of(lax.rem(y + step[0], NY), lax.rem(z + step[1], NZ)) > mine

    sibling = (s + 1 - 2 * core, x)
    barrier = pltpu.get_barrier_semaphore()
    other = [(s + 1 - 2 * core, lax.rem(x + k, NX)) for k in (1, 2, 3)]
    near = [along_x(k) for k in (1, 2, 3)] + [sibling] + other
    for peer in near:
        pl.semaphore_signal(barrier, inc=1, device_id=peer, device_id_type=MESH)

    for step in L2_STEPS + L3_STEPS:

        @pl.when(later(step))
        def _():
            pl.semaphore_signal(barrier, inc=1, device_id=along_seq(step), device_id_type=MESH)

    own_offs = pltpu.make_async_copy(offs, osm, own_sem.at[2])
    own_offs.start()
    loads = [pltpu.make_async_copy(qkv.at[i], xin.at[i], in_sem.at[i]) for i in range(3)]
    for load in loads:
        load.start()

    n_later = jnp.int32(0)
    for step in L2_STEPS + L3_STEPS:
        n_later = n_later + jnp.where(later(step), 1, 0)
    n_earlier = len(L2_STEPS + L3_STEPS) - n_later

    sends = []

    def send(src, dst, send_sem, recv_sem, peer):
        copy = pltpu.make_async_remote_copy(
            src_ref=src, dst_ref=dst, send_sem=send_sem, recv_sem=recv_sem, device_id=peer, device_id_type=MESH
        )
        copy.start()
        sends.append(copy)
        return copy

    a, b = iota((ROWS, ROWS), 0), iota((ROWS, ROWS), 1)
    forth = jnp.where(b == source_row(a), 1.0, 0.0).astype(BF)
    perm[...] = forth
    low = lanes_low((ROWS, 128))
    low_half = lanes_low((128, 128))

    own_offs.wait()
    for i in range(GH):
        sm[x, i] = osm[i]
    pl.semaphore_wait(barrier, len(near) + n_earlier)
    o_copies = [
        [
            pltpu.make_async_remote_copy(
                src_ref=sm.at[x], dst_ref=sm.at[x], send_sem=o_send.at[c, k - 1], recv_sem=o_recv.at[k - 1],
                device_id=(s - core + c, lax.rem(x + k, NX)), device_id_type=MESH,
            )
            for k in (1, 2, 3)
        ]
        for c in (0, 1)
    ]

    @pl.when(core == 1)
    def _():
        for k in (3, 1, 2):
            for c in (0, 1):
                o_copies[c][k - 1].start()


    loads[0].wait()
    forth_scaled = forth * jnp.asarray(HD**-0.5, BF)
    for t in range(3):
        wide = dot(forth_scaled, xin[0, :, t * 256 : (t + 1) * 256])
        for u in range(4):
            head = 4 * t + u
            tile = wide[:, u // 2 * 128 : (u // 2 + 1) * 128]
            first, second = tile[:128], tile[128:]
            if u % 2 == 0:
                packed = jnp.where(low_half, first, pltpu.roll(second, HD, 1))
            else:
                packed = jnp.where(low_half, pltpu.roll(first, HD, 1), second)
            qs[head // GH, head % GH] = packed.astype(BF)

    def send_q(hh):
        return [
            send(qs.at[lax.rem(x + k, NX), hh], qr.at[hh, x], q_send.at[hh, k - 1], q_recv.at[hh, k - 1], along_x(k))
            for k in (1, 3, 2)
        ]

    q_copies = [send_q(0)]
    for step in L2_STEPS + L3_STEPS:

        @pl.when(jnp.logical_not(later(step)))
        def _():
            pl.semaphore_signal(ready, inc=1, device_id=along_seq(step), device_id_type=MESH)

    own_q = pltpu.make_async_copy(qs.at[x], qr.at[:, x], own_sem.at[0])
    own_q.start()

    loads[1].wait()
    loads[2].wait()
    for t in range(6):
        both = jnp.concatenate(
            [xin[1, :, t * 128 : (t + 1) * 128], xin[2, :, t * 128 : (t + 1) * 128]], axis=1
        )
        wide = dot(forth, both)
        keys, values = wide[:, :128], wide[:, 128:]
        even = jnp.where(low, keys, pltpu.roll(values, HD, 1))
        odd = jnp.where(low, pltpu.roll(keys, HD, 1), values)
        for head, packed in ((2 * t, even), (2 * t + 1, odd)):
            kvs[head // GH, head % GH] = packed.astype(BF)

    def pick_first(g):
        for hh in range(GH):
            b0, b1, b2, b3 = bits(sm[g, hh], (16, 128))
            parts = [kvs[g, hh, i * 16 : (i + 1) * 16, :] for i in range(16)]
            kvrel[g, hh, 0:16, :] = pick([pick(parts[i::4], b0, b1) for i in range(4)], b2, b3)

    def send_rows_to(k, first, count, send_sem, recv_sem):
        return send(
            kvrel.at[lax.rem(x + k, NX), :, pl.ds(first, count), :], kv.at[:, x, pl.ds(first, count), :],
            send_sem.at[k - 1], recv_sem.at[k - 1], along_x(k),
        )

    def keep_rows(first, count, sem):
        own = pltpu.make_async_copy(
            kvrel.at[x, :, pl.ds(first, count), :], kv.at[:, x, pl.ds(first, count), :], sem
        )
        own.start()
        return own

    pick_first(x)
    own_s = keep_rows(0, 16, own_sem.at[3])
    s_copies = []
    for k in (1, 3, 2):
        o_copies[0][3 - k].wait_recv()
        pick_first(lax.rem(x + k, NX))
        s_copies.append(send_rows_to(k, 0, 16, s_send, s_recv))
    for g in range(NX):
        for hh in range(GH):
            b0, b1, b2, b3 = bits(sm[g, hh], (16, 128))
            parts = [kvs[g, hh, i * 16 : (i + 1) * 16, :] for i in range(16)]
            parts = turn(turn(parts, b0, 4), b1, 8)
            parts[:4] = turn(turn(parts[:4], b2, 1), b3, 2)
            for i in range(1, 16):
                kvrel[g, hh, i * 16 : (i + 1) * 16, :] = parts[i]
    u_copies = [send_rows_to(k, 16, 48, u_send, u_recv) for k in (1, 3, 2)]
    own_u = keep_rows(16, 48, own_sem.at[4])
    q_copies += [send_q(1), send_q(2)]
    r_copies = [
        [
            send(
                kvrel.at[lax.rem(x + k, NX), hh, pl.ds(64, 192), :], kv.at[hh, x, pl.ds(64, 192), :],
                r_send.at[hh, k - 1], r_recv.at[hh, k - 1], along_x(k),
            )
            for k in (1, 3, 2)
        ]
        for hh in range(GH)
    ]
    own_r = keep_rows(64, 192, own_sem.at[1])

    digits = []
    for hh in range(GH):
        o = sm[x, hh]
        digits.append((o & 3, (o >> 2) & 3, (o >> 4) & 3))

    own_s.wait()
    for copy in s_copies:
        copy.wait_recv()
    e_row, e_col = iota((16, 64), 0), iota((16, 64), 1)
    for hh in range(GH):
        chosen = jnp.where(e_col == ((e_row & 12) << 2) + digits[hh][2] * 4 + (e_row & 3), 1.0, 0.0).astype(BF)
        k3own[hh] = dot(chosen, kv[hh, :, 0:16, :].reshape(64, 128)).astype(BF)

    @pl.when(n_later > 0)
    def _():
        pl.semaphore_wait(ready, n_later)

    l3_copies = [
        send(k3own, k3.at[i], l3_send.at[i], l3_recv.at[i], along_seq(step)) for i, step in enumerate(L3_STEPS)
    ]
    l2_copies = [
        send(kv.at[:, :, pl.ds(0, 16), :], k2.at[i], l2_send.at[i], l2_recv.at[i], along_seq(step))
        for i, step in enumerate(L2_STEPS)
    ]
    own_u.wait()
    for copy in u_copies:
        copy.wait_recv()
    c_copy = send(kv.at[:, :, pl.ds(0, 64), :], k1s, c_send, c_recv, sibling)

    own_q.wait()
    for hh in range(GH):
        for copy in q_copies[hh]:
            copy.wait_recv()
        for j in range(NX):
            tile = qr[hh, j].astype(F32)
            qz[hh, j, 0:128, :] = jnp.where(low_half, tile, 0.0).astype(BF)
            qz[hh, j, 128:256, :] = jnp.where(low_half, pltpu.roll(tile, HD, 1), 0.0).astype(BF)

    c_copy.wait_recv()
    keys, values, scores = [], [], []
    for hh in range(GH):
        b0, b1, b2, b3 = bits(sm[x, hh], (16, 128))
        q1 = []
        for j in range(NX):
            parts = [qz[hh, j, i * 16 : (i + 1) * 16, :] for i in range(16)]
            chosen = [pick(parts[i::4], b0, b1) for i in range(4)]
            q1 += chosen
            q2s[hh, j] = pick(chosen, b2, b3)
        q1 = jnp.concatenate(q1, axis=0)
        keys.append(jnp.concatenate([kv[hh, :, 0:64, :].reshape(256, 128), k1s[hh].reshape(256, 128)], axis=0))
        scores.append(dot_t(q1, keys[hh]))
    soft = [soften(scores[hh]) for hh in range(GH)]
    for hh in range(GH):
        n1[hh] = dot(soft[hh][0], ones_and_values(keys[hh]))
        t1[hh] = soft[hh][1]

    own_r.wait()
    for hh in range(GH):
        for copy in r_copies[hh]:
            copy.wait_recv()
        keys = [kv[hh, 2 * seg : 2 * seg + 2].reshape(512, 128) for seg in range(2)]
        values = [ones_and_values(keys[seg]) for seg in range(2)]
        for pair in ((0, 2), (1, 3)):
            scores = [dot_t(qz[hh, j], keys[j // 2]) for j in pair]
            soft = [soften(scores[i]) for i in range(2)]
            nums = [dot(soft[i][0], values[pair[i] // 2]) for i in range(2)]
            for i, j in enumerate(pair):
                n0[hh, j] = nums[i]
                t0[hh, j] = soft[i][1]
                value = quotient(nums[i], hh % 2 == 0).astype(BF)
                if hh % 2 == 1:
                    value = jnp.where(low, outp[j, :, 0:128], value)
                outp[j, :, hh // 2 * 128 : (hh // 2 + 1) * 128] = value
        if hh == 0:
            for copy in l2_copies:
                copy.wait_recv()
            f2_copy = send(k2.at[pl.ds(0, N2)], k2.at[pl.ds(N2, N2)], f_send.at[0], f_recv.at[0], sibling)
        if hh == 1:
            for copy in l3_copies:
                copy.wait_recv()
            f3_copy = send(k3.at[pl.ds(0, N3)], k3.at[pl.ds(N3, N3)], f_send.at[1], f_recv.at[1], sibling)

    f2_copy.wait_recv()
    scores = []
    for hh in range(GH):
        keys2 = jnp.concatenate(
            [kv[hh, :, 0:16, :].reshape(64, 128), k1s[hh, :, 0:16, :].reshape(64, 128)]
            + [k2[i, hh].reshape(64, 128) for i in range(2 * N2)],
            axis=0,
        )
        scores.append(dot_t(q2s[hh].reshape(64, 128), keys2))
        s2[hh] = scores[hh]
        v2[hh] = ones_and_values(keys2)
    soft = [soften(scores[hh]) for hh in range(GH)]
    for hh in range(GH):
        n2[hh] = dot(soft[hh][0], v2[hh])
        t2[hh] = soft[hh][1]

    f3_copy.wait_recv()
    col = iota((64, 512), 1)
    row64 = iota((64, 1), 0)
    row256 = iota((ROWS, 1), 0)
    low16 = lanes_low((16, 128))
    keys = [jnp.concatenate([k3[i, hh] for i in range(2 * N3)], axis=0) for hh in range(GH)]
    scores = [dot_t(q2s[hh].reshape(64, 128), keys[hh]) for hh in range(GH)]
    soft = [
        soften(jnp.concatenate([jnp.where(((col >> 2) & 3) == digits[hh][2], s2[hh], LOW), scores[hh]], axis=1))
        for hh in range(GH)
    ]
    num3 = [
        dot(soft[hh][0][:, :512], v2[hh]) + dot(soft[hh][0][:, 512:], ones_and_values(keys[hh]))
        for hh in range(GH)
    ]
    both = [
        merge(n2[hh], t2[hh], num3[hh], jnp.where(((row64 >> 2) & 3) == digits[hh][2], soft[hh][1], LOW))
        for hh in range(GH)
    ]
    both = [
        merge(
            n1[hh], t1[hh], spread(both[hh][0], 16),
            jnp.where(((row256 >> 4) & 3) == digits[hh][1], spread(both[hh][1], 16), LOW),
        )
        for hh in range(GH)
    ]
    for hh in range(GH):
        c1 = digits[hh][0]
        num1, top1 = both[hh]
        b0, b1, _, _ = bits(sm[x, hh], (64, 128))
        part = jnp.concatenate(
            [pick([n0[hh, j, i * 64 : (i + 1) * 64, :] for i in range(4)], b0, b1) for j in range(NX)], axis=0
        )
        b0, b1, _, _ = bits(sm[x, hh], (64, 1))
        part_top = jnp.concatenate(
            [pick([t0[hh, j, i * 64 : (i + 1) * 64, :] for i in range(4)], b0, b1) for j in range(NX)], axis=0
        )
        num, _ = merge(part, part_top, num1, top1)
        value = quotient(num, hh % 2 == 0).astype(BF)
        place = jnp.zeros((16, 128), jnp.int32) + c1
        side = [low16, jnp.logical_not(low16), low16][hh]
        masks = [(place == i) & side for i in range(4)]
        lanes = slice(hh // 2 * 128, (hh // 2 + 1) * 128)
        for j in range(NX):
            for i in range(16):
                new = value[j * 64 + i % 4 * 16 : j * 64 + i % 4 * 16 + 16]
                rows = slice(i * 16, (i + 1) * 16)
                outp[j, rows, lanes] = jnp.where(masks[i // 4], new, outp[j, rows, lanes])
    for j in range(NX):
        final = lax.dot_general(
            outp[j], perm[...], (((0,), (0,)), ((), ())), preferred_element_type=F32
        )
        out[:, j * ROWS : (j + 1) * ROWS] = final[: GH * HD].astype(BF)

    for copy in sends:
        copy.wait_send()

    @pl.when(core == 1)
    def _():
        for copy in o_copies[0] + o_copies[1]:
            copy.wait_send()


def per_device(qkv, offsets):
    dma = pltpu.SemaphoreType.DMA
    turned = pl.pallas_call(
        kernel,
        out_shape=jax.ShapeDtypeStruct((GH * HD, NX * ROWS), BF),
        in_specs=[pl.BlockSpec(memory_space=pltpu.HBM), pl.BlockSpec(memory_space=pltpu.HBM)],
        out_specs=pl.BlockSpec(memory_space=pltpu.VMEM),
        scratch_shapes=[
            pltpu.VMEM((3, ROWS, 768), BF),
            pltpu.VMEM((ROWS, ROWS), BF),
            pltpu.VMEM((NX, GH, 128, 128), BF),
            pltpu.VMEM((NX, GH, ROWS, 128), BF),
            pltpu.VMEM((NX, GH, ROWS, 128), BF),
            pltpu.VMEM((GH, NX, 128, 128), BF),
            pltpu.VMEM((GH, NX, ROWS, 128), BF),
            pltpu.VMEM((GH, NX, ROWS, 128), BF),
            pltpu.VMEM((GH, NX, 64, 128), BF),
            pltpu.VMEM((GH, NX, 16, 128), BF),
            pltpu.VMEM((2 * N2, GH, NX, 16, 128), BF),
            pltpu.VMEM((GH, 16, 128), BF),
            pltpu.VMEM((2 * N3, GH, 16, 128), BF),
            pltpu.SMEM((GH,), jnp.int32),
            pltpu.SMEM((NX, 128), jnp.int32),
            pltpu.VMEM((GH, NX, ROWS, 128), F32),
            pltpu.VMEM((GH, NX, ROWS, 1), F32),
            pltpu.VMEM((GH, ROWS, 128), F32),
            pltpu.VMEM((GH, ROWS, 1), F32),
            pltpu.VMEM((GH, 64, 512), F32),
            pltpu.VMEM((GH, 512, 128), BF),
            pltpu.VMEM((GH, 64, 128), F32),
            pltpu.VMEM((GH, 64, 1), F32),
            pltpu.VMEM((NX, ROWS, 256), BF),
            dma((3,)), dma((8,)), dma((2, 3)), dma((3,)), dma((GH, 3)), dma((GH, 3)), dma((3,)), dma((3,)),
            dma((3,)), dma((3,)), dma((GH, 3)), dma((GH, 3)), dma, dma, dma((N2,)), dma((N2,)), dma((N3,)), dma((N3,)),
            dma((2,)), dma((2,)),
            pltpu.SemaphoreType.REGULAR,
        ],
        compiler_params=pltpu.CompilerParams(
            collective_id=0, has_side_effects=True, vmem_limit_bytes=40 * 2**20
        ),
        cost_estimate=pl.CostEstimate(flops=10**9, bytes_accessed=2 * 10**6, transcendentals=2 * 10**6),
    )(pltpu.with_memory_space_constraint(qkv, pltpu.HBM), pltpu.with_memory_space_constraint(offsets, pltpu.HBM))
    return turned.T


def solution(mesh):
    return jax.shard_map(
        per_device,
        mesh=mesh,
        in_specs=(P(None, ("seq", "head"), None), P("head")),
        out_specs=P("seq", "head"),
        check_vma=False,
    )
```

```python
import jax
import jax.numpy as jnp
from jax import lax
from jax.experimental import pallas as pl
from jax.experimental.pallas import tpu as pltpu
from jax.sharding import PartitionSpec as P

HD = 64
GH = 3
NX = 4
NY = 4
NZ = 4
ROWS = 256
MESH = pl.DeviceIdType.MESH
LOW = -1.0e30
BF = jnp.bfloat16
F32 = jnp.float32

L2_STEPS = [(0, dz) for dz in (2, 1, 3)]
L3_STEPS = [(dy, dz) for dy in (2, 1, 3) for dz in (2, 1, 3, 0)]
N2, N3 = len(L2_STEPS), len(L3_STEPS)


def iota(shape, dim):
    return lax.broadcasted_iota(jnp.int32, shape, dim)


def dot(a, b):
    return jnp.dot(a, b, preferred_element_type=F32)


def dot_t(a, b):
    return lax.dot_general(a, b, (((1,), (1,)), ((), ())), preferred_element_type=F32)


def source_row(i):
    return ((i & 3) << 6) | ((i & 12) << 2) | ((i & 48) >> 2) | (i >> 6)


def bits(o, shape):
    spread_out = jnp.zeros(shape, jnp.int32) + o
    return [(spread_out >> i) & 1 == 1 for i in range(4)]


def turn(parts, mask, step):
    return [jnp.where(mask, parts[(i + step) % len(parts)], part) for i, part in enumerate(parts)]


def pick(four, low_bit, high_bit):
    return jnp.where(high_bit, jnp.where(low_bit, four[3], four[2]), jnp.where(low_bit, four[1], four[0]))


def lanes_low(shape):
    return iota(shape, 1) < HD


def soften(scores):
    top = jnp.max(scores, axis=1, keepdims=True)
    return jnp.exp(scores - top).astype(BF), top


def ones_and_values(kv):
    return jnp.where(lanes_low(kv.shape), jnp.ones_like(kv), kv)


def merge(a, a_top, b, b_top):
    top = jnp.maximum(a_top, b_top)
    return a * jnp.exp(a_top - top) + b * jnp.exp(b_top - top), top


def quotient(num, low_side):
    turned = pltpu.roll(num, HD, 1)
    return turned / num if low_side else num / turned


def order_of(y, z):
    corner = jnp.where((z == 3) & (y == 0), 4, 0) + jnp.where((z == 0) & (y == 3), 6, 0)
    return (8 * z + 7 * jnp.minimum(y, 2) + jnp.where(y == 3, 1, 0) - corner) * 4 + y


def kernel(
    qkv, offs, out,
    xin, perm, qs, kvs, kvrel, qr, qz, kv, k1s, q2s, k2, k3own, k3, osm, sm, n0, t0, n1, t1, nm, tm, s2, v2, n2, t2, outp,
    in_sem, own_sem, o_send, o_recv, q_send, q_recv, s_send, s_recv, u_send, u_recv, r_send, r_recv,
    c_send, c_recv, l2_send, l2_recv, l3_send, l3_recv, f_send, f_recv, ready,
):
    s = lax.axis_index("seq")
    x = lax.axis_index("head")
    core, z, y = lax.rem(s, 2), lax.rem(lax.div(s, 2), NZ), lax.div(s, 2 * NZ)

    def along_x(k):
        return (s, lax.rem(x + k, NX))

    def along_seq(step):
        return (lax.rem(y + step[0], NY) * (2 * NZ) + lax.rem(z + step[1], NZ) * 2 + core, x)

    mine = order_of(y, z)

    def later(step):
        return order_of(lax.rem(y + step[0], NY), lax.rem(z + step[1], NZ)) > mine

    sibling = (s + 1 - 2 * core, x)
    barrier = pltpu.get_barrier_semaphore()
    other = [(s + 1 - 2 * core, lax.rem(x + k, NX)) for k in (1, 2, 3)]
    near = [along_x(k) for k in (1, 2, 3)] + [sibling] + other
    for peer in near:
        pl.semaphore_signal(barrier, inc=1, device_id=peer, device_id_type=MESH)

    for step in L2_STEPS + L3_STEPS:

        @pl.when(later(step))
        def _():
            pl.semaphore_signal(barrier, inc=1, device_id=along_seq(step), device_id_type=MESH)

    own_offs = pltpu.make_async_copy(offs, osm, own_sem.at[2])
    own_offs.start()
    loads = [pltpu.make_async_copy(qkv.at[i], xin.at[i], in_sem.at[i]) for i in range(3)]
    for load in loads:
        load.start()

    n_later = jnp.int32(0)
    for step in L2_STEPS + L3_STEPS:
        n_later = n_later + jnp.where(later(step), 1, 0)
    n_earlier = len(L2_STEPS + L3_STEPS) - n_later

    sends = []

    def send(src, dst, send_sem, recv_sem, peer):
        copy = pltpu.make_async_remote_copy(
            src_ref=src, dst_ref=dst, send_sem=send_sem, recv_sem=recv_sem, device_id=peer, device_id_type=MESH
        )
        copy.start()
        sends.append(copy)
        return copy

    a, b = iota((ROWS, ROWS), 0), iota((ROWS, ROWS), 1)
    forth = jnp.where(b == source_row(a), 1.0, 0.0).astype(BF)
    perm[...] = forth
    low = lanes_low((ROWS, 128))
    low_half = lanes_low((128, 128))

    loads[0].wait()
    forth_scaled = forth * jnp.asarray(HD**-0.5, BF)
    for t in range(3):
        wide = dot(forth_scaled, xin[0, :, t * 256 : (t + 1) * 256])
        for u in range(4):
            head = 4 * t + u
            tile = wide[:, u // 2 * 128 : (u // 2 + 1) * 128]
            first, second = tile[:128], tile[128:]
            if u % 2 == 0:
                packed = jnp.where(low_half, first, pltpu.roll(second, HD, 1))
            else:
                packed = jnp.where(low_half, pltpu.roll(first, HD, 1), second)
            qs[head // GH, head % GH] = packed.astype(BF)

    own_offs.wait()
    for i in range(GH):
        sm[x, i] = osm[i]
    pl.semaphore_wait(barrier, len(near) + n_earlier)
    o_copies = [
        [
            pltpu.make_async_remote_copy(
                src_ref=sm.at[x], dst_ref=sm.at[x], send_sem=o_send.at[c, k - 1], recv_sem=o_recv.at[k - 1],
                device_id=(s - core + c, lax.rem(x + k, NX)), device_id_type=MESH,
            )
            for k in (1, 2, 3)
        ]
        for c in (0, 1)
    ]

    @pl.when(core == 1)
    def _():
        for k in (3, 1, 2):
            for c in (0, 1):
                o_copies[c][k - 1].start()


    def send_q(hh):
        return [
            send(qs.at[lax.rem(x + k, NX), hh], qr.at[hh, x], q_send.at[hh, k - 1], q_recv.at[hh, k - 1], along_x(k))
            for k in (1, 3, 2)
        ]

    q_copies = [send_q(0), send_q(1)]
    for step in L2_STEPS + L3_STEPS:

        @pl.when(jnp.logical_not(later(step)))
        def _():
            pl.semaphore_signal(ready, inc=1, device_id=along_seq(step), device_id_type=MESH)

    own_q = pltpu.make_async_copy(qs.at[x], qr.at[:, x], own_sem.at[0])
    own_q.start()

    loads[1].wait()
    loads[2].wait()
    for t in range(6):
        both = jnp.concatenate(
            [xin[1, :, t * 128 : (t + 1) * 128], xin[2, :, t * 128 : (t + 1) * 128]], axis=1
        )
        wide = dot(forth, both)
        keys, values = wide[:, :128], wide[:, 128:]
        even = jnp.where(low, keys, pltpu.roll(values, HD, 1))
        odd = jnp.where(low, pltpu.roll(keys, HD, 1), values)
        for head, packed in ((2 * t, even), (2 * t + 1, odd)):
            kvs[head // GH, head % GH] = packed.astype(BF)

    def pick_first(g):
        for hh in range(GH):
            b0, b1, b2, b3 = bits(sm[g, hh], (16, 128))
            parts = [kvs[g, hh, i * 16 : (i + 1) * 16, :] for i in range(16)]
            kvrel[g, hh, 0:16, :] = pick([pick(parts[i::4], b0, b1) for i in range(4)], b2, b3)

    def send_rows_to(k, first, count, send_sem, recv_sem):
        return send(
            kvrel.at[lax.rem(x + k, NX), :, pl.ds(first, count), :], kv.at[:, x, pl.ds(first, count), :],
            send_sem.at[k - 1], recv_sem.at[k - 1], along_x(k),
        )

    def keep_rows(first, count, sem):
        own = pltpu.make_async_copy(
            kvrel.at[x, :, pl.ds(first, count), :], kv.at[:, x, pl.ds(first, count), :], sem
        )
        own.start()
        return own

    pick_first(x)
    own_s = keep_rows(0, 16, own_sem.at[3])
    s_copies = []
    for k in (1, 3, 2):
        o_copies[0][3 - k].wait_recv()
        pick_first(lax.rem(x + k, NX))
        s_copies.append(send_rows_to(k, 0, 16, s_send, s_recv))
    for g in range(NX):
        for hh in range(GH):
            b0, b1, b2, b3 = bits(sm[g, hh], (16, 128))
            parts = [kvs[g, hh, i * 16 : (i + 1) * 16, :] for i in range(16)]
            parts = turn(turn(parts, b0, 4), b1, 8)
            parts[:4] = turn(turn(parts[:4], b2, 1), b3, 2)
            for i in range(1, 16):
                kvrel[g, hh, i * 16 : (i + 1) * 16, :] = parts[i]
    u_copies = [send_rows_to(k, 16, 48, u_send, u_recv) for k in (1, 3, 2)]
    own_u = keep_rows(16, 48, own_sem.at[4])
    q_copies += [send_q(2)]
    r_copies = [
        [
            send(
                kvrel.at[lax.rem(x + k, NX), hh, pl.ds(64, 192), :], kv.at[hh, x, pl.ds(64, 192), :],
                r_send.at[hh, k - 1], r_recv.at[hh, k - 1], along_x(k),
            )
            for k in (1, 3, 2)
        ]
        for hh in range(GH)
    ]
    own_r = keep_rows(64, 192, own_sem.at[1])

    digits = []
    for hh in range(GH):
        o = sm[x, hh]
        digits.append((o & 3, (o >> 2) & 3, (o >> 4) & 3))

    own_s.wait()
    for copy in s_copies:
        copy.wait_recv()
    e_row, e_col = iota((16, 64), 0), iota((16, 64), 1)
    for hh in range(GH):
        chosen = jnp.where(e_col == ((e_row & 12) << 2) + digits[hh][2] * 4 + (e_row & 3), 1.0, 0.0).astype(BF)
        k3own[hh] = dot(chosen, kv[hh, :, 0:16, :].reshape(64, 128)).astype(BF)

    @pl.when(n_later > 0)
    def _():
        pl.semaphore_wait(ready, n_later)

    l2_copies = [
        send(kv.at[:, :, pl.ds(0, 16), :], k2.at[i], l2_send.at[i], l2_recv.at[i], along_seq(step))
        for i, step in enumerate(L2_STEPS)
    ]
    l3_copies = [
        send(k3own, k3.at[i], l3_send.at[i], l3_recv.at[i], along_seq(step)) for i, step in enumerate(L3_STEPS)
    ]
    own_u.wait()
    for copy in u_copies:
        copy.wait_recv()
    c_copy = send(kv.at[:, :, pl.ds(0, 64), :], k1s, c_send, c_recv, sibling)

    own_q.wait()
    for hh in range(GH):
        for copy in q_copies[hh]:
            copy.wait_recv()
        for j in range(NX):
            tile = qr[hh, j].astype(F32)
            qz[hh, j, 0:128, :] = jnp.where(low_half, tile, 0.0).astype(BF)
            qz[hh, j, 128:256, :] = jnp.where(low_half, pltpu.roll(tile, HD, 1), 0.0).astype(BF)

    c_copy.wait_recv()
    keys, values, scores = [], [], []
    for hh in range(GH):
        b0, b1, b2, b3 = bits(sm[x, hh], (16, 128))
        q1 = []
        for j in range(NX):
            parts = [qz[hh, j, i * 16 : (i + 1) * 16, :] for i in range(16)]
            chosen = [pick(parts[i::4], b0, b1) for i in range(4)]
            q1 += chosen
            q2s[hh, j] = pick(chosen, b2, b3)
        q1 = jnp.concatenate(q1, axis=0)
        keys.append(jnp.concatenate([kv[hh, :, 0:64, :].reshape(256, 128), k1s[hh].reshape(256, 128)], axis=0))
        scores.append(dot_t(q1, keys[hh]))
    soft = [soften(scores[hh]) for hh in range(GH)]
    for hh in range(GH):
        n1[hh] = dot(soft[hh][0], ones_and_values(keys[hh]))
        t1[hh] = soft[hh][1]

    own_r.wait()
    low16 = lanes_low((16, 128))
    for hh in range(GH):
        for copy in r_copies[hh]:
            copy.wait_recv()
        keys = [kv[hh, 2 * seg : 2 * seg + 2].reshape(512, 128) for seg in range(2)]
        values = [ones_and_values(keys[seg]) for seg in range(2)]
        for pair in ((0, 2), (1, 3)):
            scores = [dot_t(qz[hh, j], keys[j // 2]) for j in pair]
            soft = [soften(scores[i]) for i in range(2)]
            nums = [dot(soft[i][0], values[pair[i] // 2]) for i in range(2)]
            for i, j in enumerate(pair):
                n0[hh, j] = nums[i]
                t0[hh, j] = soft[i][1]
                value = quotient(nums[i], hh % 2 == 0).astype(BF)
                if hh % 2 == 1:
                    value = jnp.where(low, outp[j, :, 0:128], value)
                outp[j, :, hh // 2 * 128 : (hh // 2 + 1) * 128] = value
        b0, b1, _, _ = bits(sm[x, hh], (64, 128))
        part = jnp.concatenate(
            [pick([n0[hh, j, i * 64 : (i + 1) * 64, :] for i in range(4)], b0, b1) for j in range(NX)], axis=0
        )
        b0, b1, _, _ = bits(sm[x, hh], (64, 1))
        part_top = jnp.concatenate(
            [pick([t0[hh, j, i * 64 : (i + 1) * 64, :] for i in range(4)], b0, b1) for j in range(NX)], axis=0
        )
        num, top = merge(part, part_top, n1[hh], t1[hh])
        nm[hh] = num
        tm[hh] = top
        value = quotient(num, hh % 2 == 0).astype(BF)
        place = jnp.zeros((16, 128), jnp.int32) + digits[hh][0]
        side = [low16, jnp.logical_not(low16), low16][hh]
        masks = [(place == i) & side for i in range(4)]
        lanes = slice(hh // 2 * 128, (hh // 2 + 1) * 128)
        for j in range(NX):
            for i in range(16):
                new = value[j * 64 + i % 4 * 16 : j * 64 + i % 4 * 16 + 16]
                rows = slice(i * 16, (i + 1) * 16)
                outp[j, rows, lanes] = jnp.where(masks[i // 4], new, outp[j, rows, lanes])
        if hh == 0:
            for copy in l2_copies:
                copy.wait_recv()
            f2_copy = send(k2.at[pl.ds(0, N2)], k2.at[pl.ds(N2, N2)], f_send.at[0], f_recv.at[0], sibling)
        if hh == 1:
            for copy in l3_copies:
                copy.wait_recv()
            f3_copy = send(k3.at[pl.ds(0, N3)], k3.at[pl.ds(N3, N3)], f_send.at[1], f_recv.at[1], sibling)
            f2_copy.wait_recv()
            scores = []
            for hb in range(GH):
                keys2 = jnp.concatenate(
                    [kv[hb, :, 0:16, :].reshape(64, 128), k1s[hb, :, 0:16, :].reshape(64, 128)]
                    + [k2[i, hb].reshape(64, 128) for i in range(2 * N2)],
                    axis=0,
                )
                scores.append(dot_t(q2s[hb].reshape(64, 128), keys2))
                s2[hb] = scores[hb]
                v2[hb] = ones_and_values(keys2)
            soft = [soften(scores[hb]) for hb in range(GH)]
            for hb in range(GH):
                n2[hb] = dot(soft[hb][0], v2[hb])
                t2[hb] = soft[hb][1]

    f3_copy.wait_recv()
    col = iota((64, 512), 1)
    row64 = iota((64, 1), 0)
    keys = [jnp.concatenate([k3[i, hh] for i in range(2 * N3)], axis=0) for hh in range(GH)]
    scores = [dot_t(q2s[hh].reshape(64, 128), keys[hh]) for hh in range(GH)]
    soft = [
        soften(jnp.concatenate([jnp.where(((col >> 2) & 3) == digits[hh][2], s2[hh], LOW), scores[hh]], axis=1))
        for hh in range(GH)
    ]
    num3 = [
        dot(soft[hh][0][:, :512], v2[hh]) + dot(soft[hh][0][:, 512:], ones_and_values(keys[hh]))
        for hh in range(GH)
    ]
    both = [
        merge(n2[hh], t2[hh], num3[hh], jnp.where(((row64 >> 2) & 3) == digits[hh][2], soft[hh][1], LOW))
        for hh in range(GH)
    ]
    for hh in range(GH):
        _, _, b2, b3 = bits(sm[x, hh], (16, 128))
        part = jnp.concatenate(
            [pick([nm[hh, j * 64 + i * 16 : j * 64 + (i + 1) * 16, :] for i in range(4)], b2, b3) for j in range(NX)],
            axis=0,
        )
        _, _, b2, b3 = bits(sm[x, hh], (16, 1))
        part_top = jnp.concatenate(
            [pick([tm[hh, j * 64 + i * 16 : j * 64 + (i + 1) * 16, :] for i in range(4)], b2, b3) for j in range(NX)],
            axis=0,
        )
        num, _ = merge(part, part_top, *both[hh])
        value = quotient(num, hh % 2 == 0).astype(BF)
        place = jnp.zeros((16, 128), jnp.int32) + (digits[hh][0] * 4 + digits[hh][1])
        side = [low16, jnp.logical_not(low16), low16][hh]
        lanes = slice(hh // 2 * 128, (hh // 2 + 1) * 128)
        for i in range(16):
            mask = (place == i) & side
            rows = slice(i * 16, (i + 1) * 16)
            for j in range(NX):
                outp[j, rows, lanes] = jnp.where(mask, value[j * 16 : (j + 1) * 16], outp[j, rows, lanes])
    for j in range(NX):
        final = lax.dot_general(
            outp[j], perm[...], (((0,), (0,)), ((), ())), preferred_element_type=F32
        )
        out[:, j * ROWS : (j + 1) * ROWS] = final[: GH * HD].astype(BF)

    for copy in sends:
        copy.wait_send()

    @pl.when(core == 1)
    def _():
        for copy in o_copies[0] + o_copies[1]:
            copy.wait_send()


def per_device(qkv, offsets):
    dma = pltpu.SemaphoreType.DMA
    turned = pl.pallas_call(
        kernel,
        out_shape=jax.ShapeDtypeStruct((GH * HD, NX * ROWS), BF),
        in_specs=[pl.BlockSpec(memory_space=pltpu.HBM), pl.BlockSpec(memory_space=pltpu.HBM)],
        out_specs=pl.BlockSpec(memory_space=pltpu.VMEM),
        scratch_shapes=[
            pltpu.VMEM((3, ROWS, 768), BF),
            pltpu.VMEM((ROWS, ROWS), BF),
            pltpu.VMEM((NX, GH, 128, 128), BF),
            pltpu.VMEM((NX, GH, ROWS, 128), BF),
            pltpu.VMEM((NX, GH, ROWS, 128), BF),
            pltpu.VMEM((GH, NX, 128, 128), BF),
            pltpu.VMEM((GH, NX, ROWS, 128), BF),
            pltpu.VMEM((GH, NX, ROWS, 128), BF),
            pltpu.VMEM((GH, NX, 64, 128), BF),
            pltpu.VMEM((GH, NX, 16, 128), BF),
            pltpu.VMEM((2 * N2, GH, NX, 16, 128), BF),
            pltpu.VMEM((GH, 16, 128), BF),
            pltpu.VMEM((2 * N3, GH, 16, 128), BF),
            pltpu.SMEM((GH,), jnp.int32),
            pltpu.SMEM((NX, 128), jnp.int32),
            pltpu.VMEM((GH, NX, ROWS, 128), F32),
            pltpu.VMEM((GH, NX, ROWS, 1), F32),
            pltpu.VMEM((GH, ROWS, 128), F32),
            pltpu.VMEM((GH, ROWS, 1), F32),
            pltpu.VMEM((GH, ROWS, 128), F32),
            pltpu.VMEM((GH, ROWS, 1), F32),
            pltpu.VMEM((GH, 64, 512), F32),
            pltpu.VMEM((GH, 512, 128), BF),
            pltpu.VMEM((GH, 64, 128), F32),
            pltpu.VMEM((GH, 64, 1), F32),
            pltpu.VMEM((NX, ROWS, 256), BF),
            dma((3,)), dma((8,)), dma((2, 3)), dma((3,)), dma((GH, 3)), dma((GH, 3)), dma((3,)), dma((3,)),
            dma((3,)), dma((3,)), dma((GH, 3)), dma((GH, 3)), dma, dma, dma((N2,)), dma((N2,)), dma((N3,)), dma((N3,)),
            dma((2,)), dma((2,)),
            pltpu.SemaphoreType.REGULAR,
        ],
        compiler_params=pltpu.CompilerParams(
            collective_id=0, has_side_effects=True, vmem_limit_bytes=40 * 2**20
        ),
        cost_estimate=pl.CostEstimate(flops=10**9, bytes_accessed=2 * 10**6, transcendentals=2 * 10**6),
    )(pltpu.with_memory_space_constraint(qkv, pltpu.HBM), pltpu.with_memory_space_constraint(offsets, pltpu.HBM))
    return turned.T


def solution(mesh):
    return jax.shard_map(
        per_device,
        mesh=mesh,
        in_specs=(P(None, ("seq", "head"), None), P("head")),
        out_specs=P("seq", "head"),
        check_vma=False,
    )
```

```python
import jax
import jax.numpy as jnp
from jax import lax
from jax.experimental import pallas as pl
from jax.experimental.pallas import tpu as pltpu
from jax.sharding import PartitionSpec as P

HD = 64
GH = 3
NX = 4
NY = 4
NZ = 4
ROWS = 256
MESH = pl.DeviceIdType.MESH
LOW = -1.0e30
BF = jnp.bfloat16
F32 = jnp.float32

L2_STEPS = [(0, dz) for dz in (2, 1, 3)]
L3_STEPS = [(dy, dz) for dy in (2, 1, 3) for dz in (2, 1, 3, 0)]
N2, N3 = len(L2_STEPS), len(L3_STEPS)


def iota(shape, dim):
    return lax.broadcasted_iota(jnp.int32, shape, dim)


def dot(a, b):
    return jnp.dot(a, b, preferred_element_type=F32)


def dot_t(a, b):
    return lax.dot_general(a, b, (((1,), (1,)), ((), ())), preferred_element_type=F32)


def source_row(i):
    return ((i & 3) << 6) | ((i & 12) << 2) | ((i & 48) >> 2) | (i >> 6)


def bits(o, shape):
    spread_out = jnp.zeros(shape, jnp.int32) + o
    return [(spread_out >> i) & 1 == 1 for i in range(4)]


def turn(parts, mask, step):
    return [jnp.where(mask, parts[(i + step) % len(parts)], part) for i, part in enumerate(parts)]


def pick(four, low_bit, high_bit):
    return jnp.where(high_bit, jnp.where(low_bit, four[3], four[2]), jnp.where(low_bit, four[1], four[0]))


def lanes_low(shape):
    return iota(shape, 1) < HD


def soften(scores):
    top = jnp.max(scores, axis=1, keepdims=True)
    return jnp.exp(scores - top).astype(BF), top


def ones_and_values(kv):
    return jnp.where(lanes_low(kv.shape), jnp.ones_like(kv), kv)


def merge(a, a_top, b, b_top):
    top = jnp.maximum(a_top, b_top)
    return a * jnp.exp(a_top - top) + b * jnp.exp(b_top - top), top


def quotient(num, low_side):
    turned = pltpu.roll(num, HD, 1)
    return turned / num if low_side else num / turned


def order_of(y, z):
    corner = jnp.where((z == 3) & (y == 0), 4, 0) + jnp.where((z == 0) & (y == 3), 6, 0)
    return (8 * z + 7 * jnp.minimum(y, 2) + jnp.where(y == 3, 1, 0) - corner) * 4 + y


def kernel(
    qkv, offs, out,
    xin, perm, qs, kvs, kvrel, qr, qz, kv, k1s, q2s, k2, k3own, k3, osm, sm, n0, t0, n1, t1, nm, tm, s2, v2, n2, t2, outp,
    in_sem, own_sem, o_send, o_recv, q_send, q_recv, s_send, s_recv, u_send, u_recv, r_send, r_recv,
    c_send, c_recv, l2_send, l2_recv, l3_send, l3_recv, f_send, f_recv, ready,
):
    s = lax.axis_index("seq")
    x = lax.axis_index("head")
    core, z, y = lax.rem(s, 2), lax.rem(lax.div(s, 2), NZ), lax.div(s, 2 * NZ)

    def along_x(k):
        return (s, lax.rem(x + k, NX))

    def along_seq(step):
        return (lax.rem(y + step[0], NY) * (2 * NZ) + lax.rem(z + step[1], NZ) * 2 + core, x)

    mine = order_of(y, z)

    def later(step):
        return order_of(lax.rem(y + step[0], NY), lax.rem(z + step[1], NZ)) > mine

    sibling = (s + 1 - 2 * core, x)
    barrier = pltpu.get_barrier_semaphore()
    other = [(s + 1 - 2 * core, lax.rem(x + k, NX)) for k in (1, 2, 3)]
    near = [along_x(k) for k in (1, 2, 3)] + [sibling] + other
    for peer in near:
        pl.semaphore_signal(barrier, inc=1, device_id=peer, device_id_type=MESH)

    for step in L2_STEPS + L3_STEPS:

        @pl.when(later(step))
        def _():
            pl.semaphore_signal(barrier, inc=1, device_id=along_seq(step), device_id_type=MESH)

    own_offs = pltpu.make_async_copy(offs, osm, own_sem.at[2])
    own_offs.start()
    loads = [pltpu.make_async_copy(qkv.at[i], xin.at[i], in_sem.at[i]) for i in range(3)]
    for load in loads:
        load.start()

    n_later = jnp.int32(0)
    for step in L2_STEPS + L3_STEPS:
        n_later = n_later + jnp.where(later(step), 1, 0)
    n_earlier = len(L2_STEPS + L3_STEPS) - n_later

    sends = []

    def send(src, dst, send_sem, recv_sem, peer):
        copy = pltpu.make_async_remote_copy(
            src_ref=src, dst_ref=dst, send_sem=send_sem, recv_sem=recv_sem, device_id=peer, device_id_type=MESH
        )
        copy.start()
        sends.append(copy)
        return copy

    a, b = iota((ROWS, ROWS), 0), iota((ROWS, ROWS), 1)
    forth = jnp.where(b == source_row(a), 1.0, 0.0).astype(BF)
    perm[...] = forth
    low = lanes_low((ROWS, 128))
    low_half = lanes_low((128, 128))

    loads[0].wait()
    forth_scaled = forth * jnp.asarray(HD**-0.5, BF)
    for t in range(3):
        wide = dot(forth_scaled, xin[0, :, t * 256 : (t + 1) * 256])
        for u in range(4):
            head = 4 * t + u
            tile = wide[:, u // 2 * 128 : (u // 2 + 1) * 128]
            first, second = tile[:128], tile[128:]
            if u % 2 == 0:
                packed = jnp.where(low_half, first, pltpu.roll(second, HD, 1))
            else:
                packed = jnp.where(low_half, pltpu.roll(first, HD, 1), second)
            qs[head // GH, head % GH] = packed.astype(BF)

    own_offs.wait()
    for i in range(GH):
        sm[x, i] = osm[i]
    pl.semaphore_wait(barrier, len(near) + n_earlier)
    o_copies = [
        [
            pltpu.make_async_remote_copy(
                src_ref=sm.at[x], dst_ref=sm.at[x], send_sem=o_send.at[c, k - 1], recv_sem=o_recv.at[k - 1],
                device_id=(s - core + c, lax.rem(x + k, NX)), device_id_type=MESH,
            )
            for k in (1, 2, 3)
        ]
        for c in (0, 1)
    ]

    @pl.when(core == 1)
    def _():
        for k in (3, 1, 2):
            for c in (0, 1):
                o_copies[c][k - 1].start()


    def send_q(hh):
        return [
            send(qs.at[lax.rem(x + k, NX), hh], qr.at[hh, x], q_send.at[hh, k - 1], q_recv.at[hh, k - 1], along_x(k))
            for k in (1, 3, 2)
        ]

    q_copies = [send_q(0), send_q(1)]
    for step in L2_STEPS + L3_STEPS:

        @pl.when(jnp.logical_not(later(step)))
        def _():
            pl.semaphore_signal(ready, inc=1, device_id=along_seq(step), device_id_type=MESH)

    own_q = pltpu.make_async_copy(qs.at[x], qr.at[:, x], own_sem.at[0])
    own_q.start()

    loads[1].wait()
    loads[2].wait()
    for t in range(6):
        both = jnp.concatenate(
            [xin[1, :, t * 128 : (t + 1) * 128], xin[2, :, t * 128 : (t + 1) * 128]], axis=1
        )
        wide = dot(forth, both)
        keys, values = wide[:, :128], wide[:, 128:]
        even = jnp.where(low, keys, pltpu.roll(values, HD, 1))
        odd = jnp.where(low, pltpu.roll(keys, HD, 1), values)
        for head, packed in ((2 * t, even), (2 * t + 1, odd)):
            kvs[head // GH, head % GH] = packed.astype(BF)

    def pick_first(g):
        for hh in range(GH):
            b0, b1, b2, b3 = bits(sm[g, hh], (16, 128))
            parts = [kvs[g, hh, i * 16 : (i + 1) * 16, :] for i in range(16)]
            kvrel[g, hh, 0:16, :] = pick([pick(parts[i::4], b0, b1) for i in range(4)], b2, b3)

    def send_rows_to(k, first, count, send_sem, recv_sem):
        return send(
            kvrel.at[lax.rem(x + k, NX), :, pl.ds(first, count), :], kv.at[:, x, pl.ds(first, count), :],
            send_sem.at[k - 1], recv_sem.at[k - 1], along_x(k),
        )

    def keep_rows(first, count, sem):
        own = pltpu.make_async_copy(
            kvrel.at[x, :, pl.ds(first, count), :], kv.at[:, x, pl.ds(first, count), :], sem
        )
        own.start()
        return own

    pick_first(x)
    own_s = keep_rows(0, 16, own_sem.at[3])
    s_copies = []
    for k in (1, 3, 2):
        o_copies[0][3 - k].wait_recv()
        pick_first(lax.rem(x + k, NX))
        s_copies.append(send_rows_to(k, 0, 16, s_send, s_recv))
    for g in range(NX):
        for hh in range(GH):
            b0, b1, b2, b3 = bits(sm[g, hh], (16, 128))
            parts = [kvs[g, hh, i * 16 : (i + 1) * 16, :] for i in range(16)]
            parts = turn(turn(parts, b0, 4), b1, 8)
            parts[:4] = turn(turn(parts[:4], b2, 1), b3, 2)
            for i in range(1, 16):
                kvrel[g, hh, i * 16 : (i + 1) * 16, :] = parts[i]
    u_copies = [send_rows_to(k, 16, 48, u_send, u_recv) for k in (1, 3, 2)]
    own_u = keep_rows(16, 48, own_sem.at[4])
    q_copies += [send_q(2)]
    r_copies = [
        [
            send(
                kvrel.at[lax.rem(x + k, NX), hh, pl.ds(64, 192), :], kv.at[hh, x, pl.ds(64, 192), :],
                r_send.at[hh, k - 1], r_recv.at[hh, k - 1], along_x(k),
            )
            for k in (1, 3, 2)
        ]
        for hh in range(GH)
    ]
    own_r = keep_rows(64, 192, own_sem.at[1])

    digits = []
    for hh in range(GH):
        o = sm[x, hh]
        digits.append((o & 3, (o >> 2) & 3, (o >> 4) & 3))

    own_s.wait()
    for copy in s_copies:
        copy.wait_recv()
    @pl.when(n_later > 0)
    def _():
        pl.semaphore_wait(ready, n_later)

    l2_copies = [
        send(kv.at[:, :, pl.ds(0, 16), :], k2.at[i], l2_send.at[i], l2_recv.at[i], along_seq(step))
        for i, step in enumerate(L2_STEPS)
    ]
    e_row, e_col = iota((16, 64), 0), iota((16, 64), 1)
    for hh in range(GH):
        chosen = jnp.where(e_col == ((e_row & 12) << 2) + digits[hh][2] * 4 + (e_row & 3), 1.0, 0.0).astype(BF)
        k3own[hh] = dot(chosen, kv[hh, :, 0:16, :].reshape(64, 128)).astype(BF)
    l3_copies = [
        send(k3own, k3.at[i], l3_send.at[i], l3_recv.at[i], along_seq(step)) for i, step in enumerate(L3_STEPS)
    ]
    own_u.wait()
    for copy in u_copies:
        copy.wait_recv()
    c_copy = send(kv.at[:, :, pl.ds(0, 64), :], k1s, c_send, c_recv, sibling)

    own_q.wait()
    for hh in range(GH):
        for copy in q_copies[hh]:
            copy.wait_recv()
        for j in range(NX):
            tile = qr[hh, j].astype(F32)
            qz[hh, j, 0:128, :] = jnp.where(low_half, tile, 0.0).astype(BF)
            qz[hh, j, 128:256, :] = jnp.where(low_half, pltpu.roll(tile, HD, 1), 0.0).astype(BF)

    c_copy.wait_recv()
    keys, values, scores = [], [], []
    for hh in range(GH):
        b0, b1, b2, b3 = bits(sm[x, hh], (16, 128))
        q1 = []
        for j in range(NX):
            parts = [qz[hh, j, i * 16 : (i + 1) * 16, :] for i in range(16)]
            chosen = [pick(parts[i::4], b0, b1) for i in range(4)]
            q1 += chosen
            q2s[hh, j] = pick(chosen, b2, b3)
        q1 = jnp.concatenate(q1, axis=0)
        keys.append(jnp.concatenate([kv[hh, :, 0:64, :].reshape(256, 128), k1s[hh].reshape(256, 128)], axis=0))
        scores.append(dot_t(q1, keys[hh]))
    soft = [soften(scores[hh]) for hh in range(GH)]
    for hh in range(GH):
        n1[hh] = dot(soft[hh][0], ones_and_values(keys[hh]))
        t1[hh] = soft[hh][1]

    own_r.wait()
    low16 = lanes_low((16, 128))
    for hh in range(GH):
        for copy in r_copies[hh]:
            copy.wait_recv()
        keys = [kv[hh, 2 * seg : 2 * seg + 2].reshape(512, 128) for seg in range(2)]
        values = [ones_and_values(keys[seg]) for seg in range(2)]
        for pair in ((0, 2), (1, 3)):
            scores = [dot_t(qz[hh, j], keys[j // 2]) for j in pair]
            soft = [soften(scores[i]) for i in range(2)]
            nums = [dot(soft[i][0], values[pair[i] // 2]) for i in range(2)]
            for i, j in enumerate(pair):
                n0[hh, j] = nums[i]
                t0[hh, j] = soft[i][1]
                value = quotient(nums[i], hh % 2 == 0).astype(BF)
                if hh % 2 == 1:
                    value = jnp.where(low, outp[j, :, 0:128], value)
                outp[j, :, hh // 2 * 128 : (hh // 2 + 1) * 128] = value
        b0, b1, _, _ = bits(sm[x, hh], (64, 128))
        part = jnp.concatenate(
            [pick([n0[hh, j, i * 64 : (i + 1) * 64, :] for i in range(4)], b0, b1) for j in range(NX)], axis=0
        )
        b0, b1, _, _ = bits(sm[x, hh], (64, 1))
        part_top = jnp.concatenate(
            [pick([t0[hh, j, i * 64 : (i + 1) * 64, :] for i in range(4)], b0, b1) for j in range(NX)], axis=0
        )
        num, top = merge(part, part_top, n1[hh], t1[hh])
        nm[hh] = num
        tm[hh] = top
        value = quotient(num, hh % 2 == 0).astype(BF)
        place = jnp.zeros((16, 128), jnp.int32) + digits[hh][0]
        side = [low16, jnp.logical_not(low16), low16][hh]
        masks = [(place == i) & side for i in range(4)]
        lanes = slice(hh // 2 * 128, (hh // 2 + 1) * 128)
        for j in range(NX):
            for i in range(16):
                new = value[j * 64 + i % 4 * 16 : j * 64 + i % 4 * 16 + 16]
                rows = slice(i * 16, (i + 1) * 16)
                outp[j, rows, lanes] = jnp.where(masks[i // 4], new, outp[j, rows, lanes])
        if hh == 0:
            for copy in l2_copies:
                copy.wait_recv()
            f2_copy = send(k2.at[pl.ds(0, N2)], k2.at[pl.ds(N2, N2)], f_send.at[0], f_recv.at[0], sibling)
        if hh == 1:
            for copy in l3_copies:
                copy.wait_recv()
            f3_copy = send(k3.at[pl.ds(0, N3)], k3.at[pl.ds(N3, N3)], f_send.at[1], f_recv.at[1], sibling)
            f2_copy.wait_recv()
            scores = []
            for hb in range(GH):
                keys2 = jnp.concatenate(
                    [kv[hb, :, 0:16, :].reshape(64, 128), k1s[hb, :, 0:16, :].reshape(64, 128)]
                    + [k2[i, hb].reshape(64, 128) for i in range(2 * N2)],
                    axis=0,
                )
                scores.append(dot_t(q2s[hb].reshape(64, 128), keys2))
                s2[hb] = scores[hb]
                v2[hb] = ones_and_values(keys2)
            soft = [soften(scores[hb]) for hb in range(GH)]
            for hb in range(GH):
                n2[hb] = dot(soft[hb][0], v2[hb])
                t2[hb] = soft[hb][1]

    f3_copy.wait_recv()
    col = iota((64, 512), 1)
    row64 = iota((64, 1), 0)
    keys = [jnp.concatenate([k3[i, hh] for i in range(2 * N3)], axis=0) for hh in range(GH)]
    scores = [dot_t(q2s[hh].reshape(64, 128), keys[hh]) for hh in range(GH)]
    soft = [
        soften(jnp.concatenate([jnp.where(((col >> 2) & 3) == digits[hh][2], s2[hh], LOW), scores[hh]], axis=1))
        for hh in range(GH)
    ]
    num3 = [
        dot(soft[hh][0][:, :512], v2[hh]) + dot(soft[hh][0][:, 512:], ones_and_values(keys[hh]))
        for hh in range(GH)
    ]
    both = [
        merge(n2[hh], t2[hh], num3[hh], jnp.where(((row64 >> 2) & 3) == digits[hh][2], soft[hh][1], LOW))
        for hh in range(GH)
    ]
    for hh in range(GH):
        _, _, b2, b3 = bits(sm[x, hh], (16, 128))
        part = jnp.concatenate(
            [pick([nm[hh, j * 64 + i * 16 : j * 64 + (i + 1) * 16, :] for i in range(4)], b2, b3) for j in range(NX)],
            axis=0,
        )
        _, _, b2, b3 = bits(sm[x, hh], (16, 1))
        part_top = jnp.concatenate(
            [pick([tm[hh, j * 64 + i * 16 : j * 64 + (i + 1) * 16, :] for i in range(4)], b2, b3) for j in range(NX)],
            axis=0,
        )
        num, _ = merge(part, part_top, *both[hh])
        value = quotient(num, hh % 2 == 0).astype(BF)
        place = jnp.zeros((16, 128), jnp.int32) + (digits[hh][0] * 4 + digits[hh][1])
        side = [low16, jnp.logical_not(low16), low16][hh]
        lanes = slice(hh // 2 * 128, (hh // 2 + 1) * 128)
        for i in range(16):
            mask = (place == i) & side
            rows = slice(i * 16, (i + 1) * 16)
            for j in range(NX):
                outp[j, rows, lanes] = jnp.where(mask, value[j * 16 : (j + 1) * 16], outp[j, rows, lanes])
    for j in range(NX):
        final = lax.dot_general(
            outp[j], perm[...], (((0,), (0,)), ((), ())), preferred_element_type=F32
        )
        out[:, j * ROWS : (j + 1) * ROWS] = final[: GH * HD].astype(BF)

    for copy in sends:
        copy.wait_send()

    @pl.when(core == 1)
    def _():
        for copy in o_copies[0] + o_copies[1]:
            copy.wait_send()


def per_device(qkv, offsets):
    dma = pltpu.SemaphoreType.DMA
    turned = pl.pallas_call(
        kernel,
        out_shape=jax.ShapeDtypeStruct((GH * HD, NX * ROWS), BF),
        in_specs=[pl.BlockSpec(memory_space=pltpu.HBM), pl.BlockSpec(memory_space=pltpu.HBM)],
        out_specs=pl.BlockSpec(memory_space=pltpu.VMEM),
        scratch_shapes=[
            pltpu.VMEM((3, ROWS, 768), BF),
            pltpu.VMEM((ROWS, ROWS), BF),
            pltpu.VMEM((NX, GH, 128, 128), BF),
            pltpu.VMEM((NX, GH, ROWS, 128), BF),
            pltpu.VMEM((NX, GH, ROWS, 128), BF),
            pltpu.VMEM((GH, NX, 128, 128), BF),
            pltpu.VMEM((GH, NX, ROWS, 128), BF),
            pltpu.VMEM((GH, NX, ROWS, 128), BF),
            pltpu.VMEM((GH, NX, 64, 128), BF),
            pltpu.VMEM((GH, NX, 16, 128), BF),
            pltpu.VMEM((2 * N2, GH, NX, 16, 128), BF),
            pltpu.VMEM((GH, 16, 128), BF),
            pltpu.VMEM((2 * N3, GH, 16, 128), BF),
            pltpu.SMEM((GH,), jnp.int32),
            pltpu.SMEM((NX, 128), jnp.int32),
            pltpu.VMEM((GH, NX, ROWS, 128), F32),
            pltpu.VMEM((GH, NX, ROWS, 1), F32),
            pltpu.VMEM((GH, ROWS, 128), F32),
            pltpu.VMEM((GH, ROWS, 1), F32),
            pltpu.VMEM((GH, ROWS, 128), F32),
            pltpu.VMEM((GH, ROWS, 1), F32),
            pltpu.VMEM((GH, 64, 512), F32),
            pltpu.VMEM((GH, 512, 128), BF),
            pltpu.VMEM((GH, 64, 128), F32),
            pltpu.VMEM((GH, 64, 1), F32),
            pltpu.VMEM((NX, ROWS, 256), BF),
            dma((3,)), dma((8,)), dma((2, 3)), dma((3,)), dma((GH, 3)), dma((GH, 3)), dma((3,)), dma((3,)),
            dma((3,)), dma((3,)), dma((GH, 3)), dma((GH, 3)), dma, dma, dma((N2,)), dma((N2,)), dma((N3,)), dma((N3,)),
            dma((2,)), dma((2,)),
            pltpu.SemaphoreType.REGULAR,
        ],
        compiler_params=pltpu.CompilerParams(
            collective_id=0, has_side_effects=True, vmem_limit_bytes=40 * 2**20
        ),
        cost_estimate=pl.CostEstimate(flops=10**9, bytes_accessed=2 * 10**6, transcendentals=2 * 10**6),
    )(pltpu.with_memory_space_constraint(qkv, pltpu.HBM), pltpu.with_memory_space_constraint(offsets, pltpu.HBM))
    return turned.T


def solution(mesh):
    return jax.shard_map(
        per_device,
        mesh=mesh,
        in_specs=(P(None, ("seq", "head"), None), P("head")),
        out_specs=P("seq", "head"),
        check_vma=False,
    )
```

```python
import jax
import jax.numpy as jnp
from jax import lax
from jax.experimental import pallas as pl
from jax.experimental.pallas import tpu as pltpu
from jax.sharding import PartitionSpec as P

HD = 64
GH = 3
NX = 4
NY = 4
NZ = 4
ROWS = 256
MESH = pl.DeviceIdType.MESH
LOW = -1.0e30
BF = jnp.bfloat16
F32 = jnp.float32

L2_STEPS = [(0, dz) for dz in (2, 1, 3)]
L3_STEPS = [(dy, dz) for dy in (2, 1, 3) for dz in (2, 1, 3, 0)]
N2, N3 = len(L2_STEPS), len(L3_STEPS)


def iota(shape, dim):
    return lax.broadcasted_iota(jnp.int32, shape, dim)


def dot(a, b):
    return jnp.dot(a, b, preferred_element_type=F32)


def dot_t(a, b):
    return lax.dot_general(a, b, (((1,), (1,)), ((), ())), preferred_element_type=F32)


def source_row(i):
    return ((i & 3) << 6) | ((i & 12) << 2) | ((i & 48) >> 2) | (i >> 6)


def bits(o, shape):
    spread_out = jnp.zeros(shape, jnp.int32) + o
    return [(spread_out >> i) & 1 == 1 for i in range(4)]


def turn(parts, mask, step):
    return [jnp.where(mask, parts[(i + step) % len(parts)], part) for i, part in enumerate(parts)]


def pick(four, low_bit, high_bit):
    return jnp.where(high_bit, jnp.where(low_bit, four[3], four[2]), jnp.where(low_bit, four[1], four[0]))


def lanes_low(shape):
    return iota(shape, 1) < HD


def soften(scores):
    top = jnp.max(scores, axis=1, keepdims=True)
    return jnp.exp(scores - top).astype(BF), top


def ones_and_values(kv):
    return jnp.where(lanes_low(kv.shape), jnp.ones_like(kv), kv)


def merge(a, a_top, b, b_top):
    top = jnp.maximum(a_top, b_top)
    return a * jnp.exp(a_top - top) + b * jnp.exp(b_top - top), top


def quotient(num, low_side):
    turned = pltpu.roll(num, HD, 1)
    return turned / num if low_side else num / turned


def order_of(y, z):
    corner = jnp.where((z == 3) & (y == 0), 4, 0) + jnp.where((z == 0) & (y == 3), 6, 0)
    return (8 * z + 7 * jnp.minimum(y, 2) + jnp.where(y == 3, 1, 0) - corner) * 4 + y


def kernel(
    qkv, offs, out,
    xin, perm, qs, kvs, kvrel, qr, qz, kv, k1s, q2s, k2, k3own, k3, osm, sm, n0, t0, n1, t1, nm, tm, s2, v2, n2, t2, outp,
    in_sem, own_sem, o_send, o_recv, q_send, q_recv, s_send, s_recv, u_send, u_recv, r_send, r_recv,
    c_send, c_recv, l2_send, l2_recv, l3_send, l3_recv, f_send, f_recv, ready,
):
    s = lax.axis_index("seq")
    x = lax.axis_index("head")
    core, z, y = lax.rem(s, 2), lax.rem(lax.div(s, 2), NZ), lax.div(s, 2 * NZ)

    def along_x(k):
        return (s, lax.rem(x + k, NX))

    def along_seq(step):
        return (lax.rem(y + step[0], NY) * (2 * NZ) + lax.rem(z + step[1], NZ) * 2 + core, x)

    mine = order_of(y, z)

    def later(step):
        return order_of(lax.rem(y + step[0], NY), lax.rem(z + step[1], NZ)) > mine

    sibling = (s + 1 - 2 * core, x)
    barrier = pltpu.get_barrier_semaphore()
    other = [(s + 1 - 2 * core, lax.rem(x + k, NX)) for k in (1, 2, 3)]
    near = [along_x(k) for k in (1, 2, 3)] + [sibling] + other
    for peer in near:
        pl.semaphore_signal(barrier, inc=1, device_id=peer, device_id_type=MESH)

    for step in L2_STEPS + L3_STEPS:

        @pl.when(later(step))
        def _():
            pl.semaphore_signal(barrier, inc=1, device_id=along_seq(step), device_id_type=MESH)

    own_offs = pltpu.make_async_copy(offs, osm, own_sem.at[2])
    own_offs.start()
    loads = [pltpu.make_async_copy(qkv.at[i], xin.at[i], in_sem.at[i]) for i in range(3)]
    for load in loads:
        load.start()

    n_later = jnp.int32(0)
    for step in L2_STEPS + L3_STEPS:
        n_later = n_later + jnp.where(later(step), 1, 0)
    n_earlier = len(L2_STEPS + L3_STEPS) - n_later

    sends = []

    def send(src, dst, send_sem, recv_sem, peer):
        copy = pltpu.make_async_remote_copy(
            src_ref=src, dst_ref=dst, send_sem=send_sem, recv_sem=recv_sem, device_id=peer, device_id_type=MESH
        )
        copy.start()
        sends.append(copy)
        return copy

    a, b = iota((ROWS, ROWS), 0), iota((ROWS, ROWS), 1)
    forth = jnp.where(b == source_row(a), 1.0, 0.0).astype(BF)
    perm[...] = forth
    low = lanes_low((ROWS, 128))
    low_half = lanes_low((128, 128))

    loads[0].wait()
    forth_scaled = forth * jnp.asarray(HD**-0.5, BF)
    for t in range(3):
        wide = dot(forth_scaled, xin[0, :, t * 256 : (t + 1) * 256])
        for u in range(4):
            head = 4 * t + u
            tile = wide[:, u // 2 * 128 : (u // 2 + 1) * 128]
            first, second = tile[:128], tile[128:]
            if u % 2 == 0:
                packed = jnp.where(low_half, first, pltpu.roll(second, HD, 1))
            else:
                packed = jnp.where(low_half, pltpu.roll(first, HD, 1), second)
            qs[head // GH, head % GH] = packed.astype(BF)

    own_offs.wait()
    for i in range(GH):
        sm[x, i] = osm[i]
    pl.semaphore_wait(barrier, len(near) + n_earlier)
    o_copies = [
        [
            pltpu.make_async_remote_copy(
                src_ref=sm.at[x], dst_ref=sm.at[x], send_sem=o_send.at[c, k - 1], recv_sem=o_recv.at[k - 1],
                device_id=(s - core + c, lax.rem(x + k, NX)), device_id_type=MESH,
            )
            for k in (1, 2, 3)
        ]
        for c in (0, 1)
    ]

    @pl.when(core == 1)
    def _():
        for k in (3, 1, 2):
            for c in (0, 1):
                o_copies[c][k - 1].start()


    def send_q(hh):
        return [
            send(qs.at[lax.rem(x + k, NX), hh], qr.at[hh, x], q_send.at[hh, k - 1], q_recv.at[hh, k - 1], along_x(k))
            for k in (1, 3, 2)
        ]

    q_copies = [send_q(0), send_q(1)]
    for step in L2_STEPS + L3_STEPS:

        @pl.when(jnp.logical_not(later(step)))
        def _():
            pl.semaphore_signal(ready, inc=1, device_id=along_seq(step), device_id_type=MESH)

    own_q = pltpu.make_async_copy(qs.at[x], qr.at[:, x], own_sem.at[0])
    own_q.start()

    loads[1].wait()
    loads[2].wait()
    for t in range(6):
        both = jnp.concatenate(
            [xin[1, :, t * 128 : (t + 1) * 128], xin[2, :, t * 128 : (t + 1) * 128]], axis=1
        )
        wide = dot(forth, both)
        keys, values = wide[:, :128], wide[:, 128:]
        even = jnp.where(low, keys, pltpu.roll(values, HD, 1))
        odd = jnp.where(low, pltpu.roll(keys, HD, 1), values)
        for head, packed in ((2 * t, even), (2 * t + 1, odd)):
            kvs[head // GH, head % GH] = packed.astype(BF)

    def pick_first(g):
        for hh in range(GH):
            b0, b1, b2, b3 = bits(sm[g, hh], (16, 128))
            parts = [kvs[g, hh, i * 16 : (i + 1) * 16, :] for i in range(16)]
            kvrel[g, hh, 0:16, :] = pick([pick(parts[i::4], b0, b1) for i in range(4)], b2, b3)

    def send_rows_to(k, first, count, send_sem, recv_sem):
        return send(
            kvrel.at[lax.rem(x + k, NX), :, pl.ds(first, count), :], kv.at[:, x, pl.ds(first, count), :],
            send_sem.at[k - 1], recv_sem.at[k - 1], along_x(k),
        )

    def keep_rows(first, count, sem):
        own = pltpu.make_async_copy(
            kvrel.at[x, :, pl.ds(first, count), :], kv.at[:, x, pl.ds(first, count), :], sem
        )
        own.start()
        return own

    pick_first(x)
    own_s = keep_rows(0, 16, own_sem.at[3])
    s_copies = []
    for k in (1, 3, 2):
        o_copies[0][3 - k].wait_recv()
        pick_first(lax.rem(x + k, NX))
        s_copies.append(send_rows_to(k, 0, 16, s_send, s_recv))
    for g in range(NX):
        for hh in range(GH):
            b0, b1, b2, b3 = bits(sm[g, hh], (16, 128))
            parts = [kvs[g, hh, i * 16 : (i + 1) * 16, :] for i in range(16)]
            parts = turn(turn(parts, b0, 4), b1, 8)
            parts[:4] = turn(turn(parts[:4], b2, 1), b3, 2)
            for i in range(1, 16):
                kvrel[g, hh, i * 16 : (i + 1) * 16, :] = parts[i]
    u_copies = [send_rows_to(k, 16, 48, u_send, u_recv) for k in (1, 3, 2)]
    own_u = keep_rows(16, 48, own_sem.at[4])
    q_copies += [send_q(2)]
    r_copies = [
        [
            send(
                kvrel.at[lax.rem(x + k, NX), hh, pl.ds(64, 192), :], kv.at[hh, x, pl.ds(64, 192), :],
                r_send.at[hh, k - 1], r_recv.at[hh, k - 1], along_x(k),
            )
            for k in (1, 3, 2)
        ]
        for hh in range(GH)
    ]
    own_r = keep_rows(64, 192, own_sem.at[1])

    digits = []
    for hh in range(GH):
        o = sm[x, hh]
        digits.append((o & 3, (o >> 2) & 3, (o >> 4) & 3))

    own_s.wait()
    for copy in s_copies:
        copy.wait_recv()
    @pl.when(n_later > 0)
    def _():
        pl.semaphore_wait(ready, n_later)

    l2_copies = [
        send(kv.at[:, :, pl.ds(0, 16), :], k2.at[i], l2_send.at[i], l2_recv.at[i], along_seq(step))
        for i, step in enumerate(L2_STEPS)
    ]
    e_row, e_col = iota((16, 64), 0), iota((16, 64), 1)
    for hh in range(GH):
        chosen = jnp.where(e_col == ((e_row & 12) << 2) + digits[hh][2] * 4 + (e_row & 3), 1.0, 0.0).astype(BF)
        k3own[hh] = dot(chosen, kv[hh, :, 0:16, :].reshape(64, 128)).astype(BF)
    l3_copies = [
        send(k3own, k3.at[i], l3_send.at[i], l3_recv.at[i], along_seq(step)) for i, step in enumerate(L3_STEPS)
    ]
    own_u.wait()
    for copy in u_copies:
        copy.wait_recv()
    c_copy = send(kv.at[:, :, pl.ds(0, 64), :], k1s, c_send, c_recv, sibling)

    own_q.wait()
    for hh in range(GH):
        for copy in q_copies[hh]:
            copy.wait_recv()
        for j in range(NX):
            tile = qr[hh, j].astype(F32)
            qz[hh, j, 0:128, :] = jnp.where(low_half, tile, 0.0).astype(BF)
            qz[hh, j, 128:256, :] = jnp.where(low_half, pltpu.roll(tile, HD, 1), 0.0).astype(BF)

    c_copy.wait_recv()
    keys, values, scores = [], [], []
    for hh in range(GH):
        b0, b1, b2, b3 = bits(sm[x, hh], (16, 128))
        q1 = []
        for j in range(NX):
            parts = [qz[hh, j, i * 16 : (i + 1) * 16, :] for i in range(16)]
            chosen = [pick(parts[i::4], b0, b1) for i in range(4)]
            q1 += chosen
            q2s[hh, j] = pick(chosen, b2, b3)
        q1 = jnp.concatenate(q1, axis=0)
        keys.append(jnp.concatenate([kv[hh, :, 0:64, :].reshape(256, 128), k1s[hh].reshape(256, 128)], axis=0))
        scores.append(dot_t(q1, keys[hh]))
    soft = [soften(scores[hh]) for hh in range(GH)]
    for hh in range(GH):
        n1[hh] = dot(soft[hh][0], ones_and_values(keys[hh]))
        t1[hh] = soft[hh][1]

    own_r.wait()
    low16 = lanes_low((16, 128))
    for hh in range(GH):
        for copy in r_copies[hh]:
            copy.wait_recv()
        keys = [kv[hh, 2 * seg : 2 * seg + 2].reshape(512, 128) for seg in range(2)]
        values = [ones_and_values(keys[seg]) for seg in range(2)]
        for pair in ((0, 1, 2, 3),):
            scores = [dot_t(qz[hh, j], keys[j // 2]) for j in pair]
            soft = [soften(scores[i]) for i in range(4)]
            nums = [dot(soft[i][0], values[pair[i] // 2]) for i in range(4)]
            for i, j in enumerate(pair):
                n0[hh, j] = nums[i]
                t0[hh, j] = soft[i][1]
                value = quotient(nums[i], hh % 2 == 0).astype(BF)
                if hh % 2 == 1:
                    value = jnp.where(low, outp[j, :, 0:128], value)
                outp[j, :, hh // 2 * 128 : (hh // 2 + 1) * 128] = value
        b0, b1, _, _ = bits(sm[x, hh], (64, 128))
        part = jnp.concatenate(
            [pick([n0[hh, j, i * 64 : (i + 1) * 64, :] for i in range(4)], b0, b1) for j in range(NX)], axis=0
        )
        b0, b1, _, _ = bits(sm[x, hh], (64, 1))
        part_top = jnp.concatenate(
            [pick([t0[hh, j, i * 64 : (i + 1) * 64, :] for i in range(4)], b0, b1) for j in range(NX)], axis=0
        )
        num, top = merge(part, part_top, n1[hh], t1[hh])
        nm[hh] = num
        tm[hh] = top
        value = quotient(num, hh % 2 == 0).astype(BF)
        place = jnp.zeros((16, 128), jnp.int32) + digits[hh][0]
        side = [low16, jnp.logical_not(low16), low16][hh]
        masks = [(place == i) & side for i in range(4)]
        lanes = slice(hh // 2 * 128, (hh // 2 + 1) * 128)
        for j in range(NX):
            for i in range(16):
                new = value[j * 64 + i % 4 * 16 : j * 64 + i % 4 * 16 + 16]
                rows = slice(i * 16, (i + 1) * 16)
                outp[j, rows, lanes] = jnp.where(masks[i // 4], new, outp[j, rows, lanes])
        if hh == 0:
            for copy in l2_copies:
                copy.wait_recv()
            f2_copy = send(k2.at[pl.ds(0, N2)], k2.at[pl.ds(N2, N2)], f_send.at[0], f_recv.at[0], sibling)
        if hh == 1:
            for copy in l3_copies:
                copy.wait_recv()
            f3_copy = send(k3.at[pl.ds(0, N3)], k3.at[pl.ds(N3, N3)], f_send.at[1], f_recv.at[1], sibling)
            f2_copy.wait_recv()
            scores = []
            for hb in range(GH):
                keys2 = jnp.concatenate(
                    [kv[hb, :, 0:16, :].reshape(64, 128), k1s[hb, :, 0:16, :].reshape(64, 128)]
                    + [k2[i, hb].reshape(64, 128) for i in range(2 * N2)],
                    axis=0,
                )
                scores.append(dot_t(q2s[hb].reshape(64, 128), keys2))
                s2[hb] = scores[hb]
                v2[hb] = ones_and_values(keys2)
            soft = [soften(scores[hb]) for hb in range(GH)]
            for hb in range(GH):
                n2[hb] = dot(soft[hb][0], v2[hb])
                t2[hb] = soft[hb][1]

    f3_copy.wait_recv()
    col = iota((64, 512), 1)
    row64 = iota((64, 1), 0)
    keys = [jnp.concatenate([k3[i, hh] for i in range(2 * N3)], axis=0) for hh in range(GH)]
    scores = [dot_t(q2s[hh].reshape(64, 128), keys[hh]) for hh in range(GH)]
    soft = [
        soften(jnp.concatenate([jnp.where(((col >> 2) & 3) == digits[hh][2], s2[hh], LOW), scores[hh]], axis=1))
        for hh in range(GH)
    ]
    num3 = [
        dot(soft[hh][0][:, :512], v2[hh]) + dot(soft[hh][0][:, 512:], ones_and_values(keys[hh]))
        for hh in range(GH)
    ]
    both = [
        merge(n2[hh], t2[hh], num3[hh], jnp.where(((row64 >> 2) & 3) == digits[hh][2], soft[hh][1], LOW))
        for hh in range(GH)
    ]
    for hh in range(GH):
        _, _, b2, b3 = bits(sm[x, hh], (16, 128))
        part = jnp.concatenate(
            [pick([nm[hh, j * 64 + i * 16 : j * 64 + (i + 1) * 16, :] for i in range(4)], b2, b3) for j in range(NX)],
            axis=0,
        )
        _, _, b2, b3 = bits(sm[x, hh], (16, 1))
        part_top = jnp.concatenate(
            [pick([tm[hh, j * 64 + i * 16 : j * 64 + (i + 1) * 16, :] for i in range(4)], b2, b3) for j in range(NX)],
            axis=0,
        )
        num, _ = merge(part, part_top, *both[hh])
        value = quotient(num, hh % 2 == 0).astype(BF)
        place = jnp.zeros((16, 128), jnp.int32) + (digits[hh][0] * 4 + digits[hh][1])
        side = [low16, jnp.logical_not(low16), low16][hh]
        lanes = slice(hh // 2 * 128, (hh // 2 + 1) * 128)
        for i in range(16):
            mask = (place == i) & side
            rows = slice(i * 16, (i + 1) * 16)
            for j in range(NX):
                outp[j, rows, lanes] = jnp.where(mask, value[j * 16 : (j + 1) * 16], outp[j, rows, lanes])
    for j in range(NX):
        final = lax.dot_general(
            outp[j], perm[...], (((0,), (0,)), ((), ())), preferred_element_type=F32
        )
        out[:, j * ROWS : (j + 1) * ROWS] = final[: GH * HD].astype(BF)

    for copy in sends:
        copy.wait_send()

    @pl.when(core == 1)
    def _():
        for copy in o_copies[0] + o_copies[1]:
            copy.wait_send()


def per_device(qkv, offsets):
    dma = pltpu.SemaphoreType.DMA
    turned = pl.pallas_call(
        kernel,
        out_shape=jax.ShapeDtypeStruct((GH * HD, NX * ROWS), BF),
        in_specs=[pl.BlockSpec(memory_space=pltpu.HBM), pl.BlockSpec(memory_space=pltpu.HBM)],
        out_specs=pl.BlockSpec(memory_space=pltpu.VMEM),
        scratch_shapes=[
            pltpu.VMEM((3, ROWS, 768), BF),
            pltpu.VMEM((ROWS, ROWS), BF),
            pltpu.VMEM((NX, GH, 128, 128), BF),
            pltpu.VMEM((NX, GH, ROWS, 128), BF),
            pltpu.VMEM((NX, GH, ROWS, 128), BF),
            pltpu.VMEM((GH, NX, 128, 128), BF),
            pltpu.VMEM((GH, NX, ROWS, 128), BF),
            pltpu.VMEM((GH, NX, ROWS, 128), BF),
            pltpu.VMEM((GH, NX, 64, 128), BF),
            pltpu.VMEM((GH, NX, 16, 128), BF),
            pltpu.VMEM((2 * N2, GH, NX, 16, 128), BF),
            pltpu.VMEM((GH, 16, 128), BF),
            pltpu.VMEM((2 * N3, GH, 16, 128), BF),
            pltpu.SMEM((GH,), jnp.int32),
            pltpu.SMEM((NX, 128), jnp.int32),
            pltpu.VMEM((GH, NX, ROWS, 128), F32),
            pltpu.VMEM((GH, NX, ROWS, 1), F32),
            pltpu.VMEM((GH, ROWS, 128), F32),
            pltpu.VMEM((GH, ROWS, 1), F32),
            pltpu.VMEM((GH, ROWS, 128), F32),
            pltpu.VMEM((GH, ROWS, 1), F32),
            pltpu.VMEM((GH, 64, 512), F32),
            pltpu.VMEM((GH, 512, 128), BF),
            pltpu.VMEM((GH, 64, 128), F32),
            pltpu.VMEM((GH, 64, 1), F32),
            pltpu.VMEM((NX, ROWS, 256), BF),
            dma((3,)), dma((8,)), dma((2, 3)), dma((3,)), dma((GH, 3)), dma((GH, 3)), dma((3,)), dma((3,)),
            dma((3,)), dma((3,)), dma((GH, 3)), dma((GH, 3)), dma, dma, dma((N2,)), dma((N2,)), dma((N3,)), dma((N3,)),
            dma((2,)), dma((2,)),
            pltpu.SemaphoreType.REGULAR,
        ],
        compiler_params=pltpu.CompilerParams(
            collective_id=0, has_side_effects=True, vmem_limit_bytes=40 * 2**20
        ),
        cost_estimate=pl.CostEstimate(flops=10**9, bytes_accessed=2 * 10**6, transcendentals=2 * 10**6),
    )(pltpu.with_memory_space_constraint(qkv, pltpu.HBM), pltpu.with_memory_space_constraint(offsets, pltpu.HBM))
    return turned.T


def solution(mesh):
    return jax.shard_map(
        per_device,
        mesh=mesh,
        in_specs=(P(None, ("seq", "head"), None), P("head")),
        out_specs=P("seq", "head"),
        check_vma=False,
    )
```

```python
import jax
import jax.numpy as jnp
from jax import lax
from jax.experimental import pallas as pl
from jax.experimental.pallas import tpu as pltpu
from jax.sharding import PartitionSpec as P

HD = 64
GH = 3
NX = 4
NY = 4
NZ = 4
ROWS = 256
MESH = pl.DeviceIdType.MESH
LOW = -1.0e30
BF = jnp.bfloat16
F32 = jnp.float32

L2_STEPS = [(0, dz) for dz in (2, 1, 3)]
L3_STEPS = [(dy, dz) for dy in (2, 1, 3) for dz in (2, 1, 3, 0)]
N2, N3 = len(L2_STEPS), len(L3_STEPS)


def iota(shape, dim):
    return lax.broadcasted_iota(jnp.int32, shape, dim)


def dot(a, b):
    return jnp.dot(a, b, preferred_element_type=F32)


def dot_t(a, b):
    return lax.dot_general(a, b, (((1,), (1,)), ((), ())), preferred_element_type=F32)


def source_row(i):
    return ((i & 3) << 6) | ((i & 12) << 2) | ((i & 48) >> 2) | (i >> 6)


def bits(o, shape):
    spread_out = jnp.zeros(shape, jnp.int32) + o
    return [(spread_out >> i) & 1 == 1 for i in range(4)]


def turn(parts, mask, step):
    return [jnp.where(mask, parts[(i + step) % len(parts)], part) for i, part in enumerate(parts)]


def pick(four, low_bit, high_bit):
    return jnp.where(high_bit, jnp.where(low_bit, four[3], four[2]), jnp.where(low_bit, four[1], four[0]))


def lanes_low(shape):
    return iota(shape, 1) < HD


def soften(scores):
    top = jnp.max(scores, axis=1, keepdims=True)
    return jnp.exp(scores - top).astype(BF), top


def ones_and_values(kv):
    return jnp.where(lanes_low(kv.shape), jnp.ones_like(kv), kv)


def merge(a, a_top, b, b_top):
    top = jnp.maximum(a_top, b_top)
    return a * jnp.exp(a_top - top) + b * jnp.exp(b_top - top), top


def quotient(num, low_side):
    turned = pltpu.roll(num, HD, 1)
    return turned / num if low_side else num / turned


def order_of(y, z):
    corner = jnp.where((z == 3) & (y == 0), 4, 0) + jnp.where((z == 0) & (y == 3), 6, 0)
    return (8 * z + 7 * jnp.minimum(y, 2) + jnp.where(y == 3, 1, 0) - corner) * 4 + y


def kernel(
    qkv, offs, out,
    xin, perm, qs, kvs, kvrel, qr, qz, kv, k1s, q2s, k2, k3own, k3, osm, sm, n0, t0, n1, t1, nm, tm, s2, v2, n2, t2, outp,
    in_sem, own_sem, o_send, o_recv, q_send, q_recv, s_send, s_recv, u_send, u_recv, r_send, r_recv,
    c_send, c_recv, l2_send, l2_recv, l3_send, l3_recv, f_send, f_recv, ready,
):
    s = lax.axis_index("seq")
    x = lax.axis_index("head")
    core, z, y = lax.rem(s, 2), lax.rem(lax.div(s, 2), NZ), lax.div(s, 2 * NZ)

    def along_x(k):
        return (s, lax.rem(x + k, NX))

    def along_seq(step):
        return (lax.rem(y + step[0], NY) * (2 * NZ) + lax.rem(z + step[1], NZ) * 2 + core, x)

    mine = order_of(y, z)

    def later(step):
        return order_of(lax.rem(y + step[0], NY), lax.rem(z + step[1], NZ)) > mine

    sibling = (s + 1 - 2 * core, x)
    barrier = pltpu.get_barrier_semaphore()
    other = [(s + 1 - 2 * core, lax.rem(x + k, NX)) for k in (1, 2, 3)]
    near = [along_x(k) for k in (1, 2, 3)] + [sibling] + other
    for peer in near:
        pl.semaphore_signal(barrier, inc=1, device_id=peer, device_id_type=MESH)

    for step in L2_STEPS + L3_STEPS:

        @pl.when(later(step))
        def _():
            pl.semaphore_signal(barrier, inc=1, device_id=along_seq(step), device_id_type=MESH)

    own_offs = pltpu.make_async_copy(offs, osm, own_sem.at[2])
    own_offs.start()
    loads = [pltpu.make_async_copy(qkv.at[i], xin.at[i], in_sem.at[i]) for i in range(3)]
    for load in loads:
        load.start()

    n_later = jnp.int32(0)
    for step in L2_STEPS + L3_STEPS:
        n_later = n_later + jnp.where(later(step), 1, 0)
    n_earlier = len(L2_STEPS + L3_STEPS) - n_later

    sends = []

    def send(src, dst, send_sem, recv_sem, peer):
        copy = pltpu.make_async_remote_copy(
            src_ref=src, dst_ref=dst, send_sem=send_sem, recv_sem=recv_sem, device_id=peer, device_id_type=MESH
        )
        copy.start()
        sends.append(copy)
        return copy

    a, b = iota((ROWS, ROWS), 0), iota((ROWS, ROWS), 1)
    forth = jnp.where(b == source_row(a), 1.0, 0.0).astype(BF)
    perm[...] = forth
    low = lanes_low((ROWS, 128))
    low_half = lanes_low((128, 128))

    loads[0].wait()
    forth_scaled = forth * jnp.asarray(HD**-0.5, BF)
    for t in range(3):
        wide = dot(forth_scaled, xin[0, :, t * 256 : (t + 1) * 256])
        for u in range(4):
            head = 4 * t + u
            tile = wide[:, u // 2 * 128 : (u // 2 + 1) * 128]
            first, second = tile[:128], tile[128:]
            if u % 2 == 0:
                packed = jnp.where(low_half, first, pltpu.roll(second, HD, 1))
            else:
                packed = jnp.where(low_half, pltpu.roll(first, HD, 1), second)
            qs[head // GH, head % GH] = packed.astype(BF)

    own_offs.wait()
    for i in range(GH):
        sm[x, i] = osm[i]
    pl.semaphore_wait(barrier, len(near) + n_earlier)
    o_copies = [
        [
            pltpu.make_async_remote_copy(
                src_ref=sm.at[x], dst_ref=sm.at[x], send_sem=o_send.at[c, k - 1], recv_sem=o_recv.at[k - 1],
                device_id=(s - core + c, lax.rem(x + k, NX)), device_id_type=MESH,
            )
            for k in (1, 2, 3)
        ]
        for c in (0, 1)
    ]

    @pl.when(core == 1)
    def _():
        for k in (3, 1, 2):
            for c in (0, 1):
                o_copies[c][k - 1].start()


    def send_q(hh):
        return [
            send(qs.at[lax.rem(x + k, NX), hh], qr.at[hh, x], q_send.at[hh, k - 1], q_recv.at[hh, k - 1], along_x(k))
            for k in (1, 3, 2)
        ]

    q_copies = [send_q(0), send_q(1)]
    own_q = pltpu.make_async_copy(qs.at[x], qr.at[:, x], own_sem.at[0])
    own_q.start()

    loads[1].wait()
    loads[2].wait()
    for t in range(6):
        both = jnp.concatenate(
            [xin[1, :, t * 128 : (t + 1) * 128], xin[2, :, t * 128 : (t + 1) * 128]], axis=1
        )
        wide = dot(forth, both)
        keys, values = wide[:, :128], wide[:, 128:]
        even = jnp.where(low, keys, pltpu.roll(values, HD, 1))
        odd = jnp.where(low, pltpu.roll(keys, HD, 1), values)
        for head, packed in ((2 * t, even), (2 * t + 1, odd)):
            kvs[head // GH, head % GH] = packed.astype(BF)

    def pick_first(g):
        for hh in range(GH):
            b0, b1, b2, b3 = bits(sm[g, hh], (16, 128))
            parts = [kvs[g, hh, i * 16 : (i + 1) * 16, :] for i in range(16)]
            kvrel[g, hh, 0:16, :] = pick([pick(parts[i::4], b0, b1) for i in range(4)], b2, b3)

    def send_rows_to(k, first, count, send_sem, recv_sem):
        return send(
            kvrel.at[lax.rem(x + k, NX), :, pl.ds(first, count), :], kv.at[:, x, pl.ds(first, count), :],
            send_sem.at[k - 1], recv_sem.at[k - 1], along_x(k),
        )

    def keep_rows(first, count, sem):
        own = pltpu.make_async_copy(
            kvrel.at[x, :, pl.ds(first, count), :], kv.at[:, x, pl.ds(first, count), :], sem
        )
        own.start()
        return own

    pick_first(x)
    own_s = keep_rows(0, 16, own_sem.at[3])
    s_copies = []
    for k in (1, 3, 2):
        o_copies[0][3 - k].wait_recv()
        pick_first(lax.rem(x + k, NX))
        s_copies.append(send_rows_to(k, 0, 16, s_send, s_recv))
    for step in L2_STEPS + L3_STEPS:

        @pl.when(jnp.logical_not(later(step)))
        def _():
            pl.semaphore_signal(ready, inc=1, device_id=along_seq(step), device_id_type=MESH)

    for g in range(NX):
        for hh in range(GH):
            b0, b1, b2, b3 = bits(sm[g, hh], (16, 128))
            parts = [kvs[g, hh, i * 16 : (i + 1) * 16, :] for i in range(16)]
            parts = turn(turn(parts, b0, 4), b1, 8)
            parts[:4] = turn(turn(parts[:4], b2, 1), b3, 2)
            for i in range(1, 16):
                kvrel[g, hh, i * 16 : (i + 1) * 16, :] = parts[i]
    u_copies = [send_rows_to(k, 16, 48, u_send, u_recv) for k in (1, 3, 2)]
    own_u = keep_rows(16, 48, own_sem.at[4])
    q_copies += [send_q(2)]
    r_copies = [
        [
            send(
                kvrel.at[lax.rem(x + k, NX), hh, pl.ds(64, 192), :], kv.at[hh, x, pl.ds(64, 192), :],
                r_send.at[hh, k - 1], r_recv.at[hh, k - 1], along_x(k),
            )
            for k in (1, 3, 2)
        ]
        for hh in range(GH)
    ]
    own_r = keep_rows(64, 192, own_sem.at[1])

    digits = []
    for hh in range(GH):
        o = sm[x, hh]
        digits.append((o & 3, (o >> 2) & 3, (o >> 4) & 3))

    own_s.wait()
    for copy in s_copies:
        copy.wait_recv()
    @pl.when(n_later > 0)
    def _():
        pl.semaphore_wait(ready, n_later)

    l2_copies = [
        send(kv.at[:, :, pl.ds(0, 16), :], k2.at[i], l2_send.at[i], l2_recv.at[i], along_seq(step))
        for i, step in enumerate(L2_STEPS)
    ]
    e_row, e_col = iota((16, 64), 0), iota((16, 64), 1)
    for hh in range(GH):
        chosen = jnp.where(e_col == ((e_row & 12) << 2) + digits[hh][2] * 4 + (e_row & 3), 1.0, 0.0).astype(BF)
        k3own[hh] = dot(chosen, kv[hh, :, 0:16, :].reshape(64, 128)).astype(BF)
    l3_copies = [
        send(k3own, k3.at[i], l3_send.at[i], l3_recv.at[i], along_seq(step)) for i, step in enumerate(L3_STEPS)
    ]
    own_u.wait()
    for copy in u_copies:
        copy.wait_recv()
    c_copy = send(kv.at[:, :, pl.ds(0, 64), :], k1s, c_send, c_recv, sibling)

    own_q.wait()
    for hh in range(GH):
        for copy in q_copies[hh]:
            copy.wait_recv()
        for j in range(NX):
            tile = qr[hh, j].astype(F32)
            qz[hh, j, 0:128, :] = jnp.where(low_half, tile, 0.0).astype(BF)
            qz[hh, j, 128:256, :] = jnp.where(low_half, pltpu.roll(tile, HD, 1), 0.0).astype(BF)

    c_copy.wait_recv()
    keys, values, scores = [], [], []
    for hh in range(GH):
        b0, b1, b2, b3 = bits(sm[x, hh], (16, 128))
        q1 = []
        for j in range(NX):
            parts = [qz[hh, j, i * 16 : (i + 1) * 16, :] for i in range(16)]
            chosen = [pick(parts[i::4], b0, b1) for i in range(4)]
            q1 += chosen
            q2s[hh, j] = pick(chosen, b2, b3)
        q1 = jnp.concatenate(q1, axis=0)
        keys.append(jnp.concatenate([kv[hh, :, 0:64, :].reshape(256, 128), k1s[hh].reshape(256, 128)], axis=0))
        scores.append(dot_t(q1, keys[hh]))
    soft = [soften(scores[hh]) for hh in range(GH)]
    for hh in range(GH):
        n1[hh] = dot(soft[hh][0], ones_and_values(keys[hh]))
        t1[hh] = soft[hh][1]

    own_r.wait()
    low16 = lanes_low((16, 128))
    for hh in range(GH):
        if hh == 2:
            done = [copy for copy in sends if all(copy is not late for late in (*r_copies[2], f2_copy, f3_copy))]
            for copy in done:
                copy.wait_send()

            @pl.when(core == 1)
            def _():
                for copy in o_copies[0] + o_copies[1]:
                    copy.wait_send()

        for copy in r_copies[hh]:
            copy.wait_recv()
        keys = [kv[hh, 2 * seg : 2 * seg + 2].reshape(512, 128) for seg in range(2)]
        values = [ones_and_values(keys[seg]) for seg in range(2)]
        for pair in ((0, 2), (1, 3)):
            scores = [dot_t(qz[hh, j], keys[j // 2]) for j in pair]
            soft = [soften(scores[i]) for i in range(2)]
            nums = [dot(soft[i][0], values[pair[i] // 2]) for i in range(2)]
            for i, j in enumerate(pair):
                n0[hh, j] = nums[i]
                t0[hh, j] = soft[i][1]
                value = quotient(nums[i], hh % 2 == 0).astype(BF)
                if hh % 2 == 1:
                    value = jnp.where(low, outp[j, :, 0:128], value)
                outp[j, :, hh // 2 * 128 : (hh // 2 + 1) * 128] = value
        b0, b1, _, _ = bits(sm[x, hh], (64, 128))
        part = jnp.concatenate(
            [pick([n0[hh, j, i * 64 : (i + 1) * 64, :] for i in range(4)], b0, b1) for j in range(NX)], axis=0
        )
        b0, b1, _, _ = bits(sm[x, hh], (64, 1))
        part_top = jnp.concatenate(
            [pick([t0[hh, j, i * 64 : (i + 1) * 64, :] for i in range(4)], b0, b1) for j in range(NX)], axis=0
        )
        num, top = merge(part, part_top, n1[hh], t1[hh])
        nm[hh] = num
        tm[hh] = top
        value = quotient(num, hh % 2 == 0).astype(BF)
        place = jnp.zeros((16, 128), jnp.int32) + digits[hh][0]
        side = [low16, jnp.logical_not(low16), low16][hh]
        masks = [(place == i) & side for i in range(4)]
        lanes = slice(hh // 2 * 128, (hh // 2 + 1) * 128)
        for j in range(NX):
            for i in range(16):
                new = value[j * 64 + i % 4 * 16 : j * 64 + i % 4 * 16 + 16]
                rows = slice(i * 16, (i + 1) * 16)
                outp[j, rows, lanes] = jnp.where(masks[i // 4], new, outp[j, rows, lanes])
        if hh == 0:
            for copy in l2_copies:
                copy.wait_recv()
            f2_copy = send(k2.at[pl.ds(0, N2)], k2.at[pl.ds(N2, N2)], f_send.at[0], f_recv.at[0], sibling)
        if hh == 1:
            for copy in l3_copies:
                copy.wait_recv()
            f3_copy = send(k3.at[pl.ds(0, N3)], k3.at[pl.ds(N3, N3)], f_send.at[1], f_recv.at[1], sibling)
            f2_copy.wait_recv()
            scores = []
            for hb in range(GH):
                keys2 = jnp.concatenate(
                    [kv[hb, :, 0:16, :].reshape(64, 128), k1s[hb, :, 0:16, :].reshape(64, 128)]
                    + [k2[i, hb].reshape(64, 128) for i in range(2 * N2)],
                    axis=0,
                )
                scores.append(dot_t(q2s[hb].reshape(64, 128), keys2))
                s2[hb] = scores[hb]
                v2[hb] = ones_and_values(keys2)
            soft = [soften(scores[hb]) for hb in range(GH)]
            for hb in range(GH):
                n2[hb] = dot(soft[hb][0], v2[hb])
                t2[hb] = soft[hb][1]

    f3_copy.wait_recv()
    col = iota((64, 512), 1)
    row64 = iota((64, 1), 0)
    keys = [jnp.concatenate([k3[i, hh] for i in range(2 * N3)], axis=0) for hh in range(GH)]
    scores = [dot_t(q2s[hh].reshape(64, 128), keys[hh]) for hh in range(GH)]
    soft = [
        soften(jnp.concatenate([jnp.where(((col >> 2) & 3) == digits[hh][2], s2[hh], LOW), scores[hh]], axis=1))
        for hh in range(GH)
    ]
    num3 = [
        dot(soft[hh][0][:, :512], v2[hh]) + dot(soft[hh][0][:, 512:], ones_and_values(keys[hh]))
        for hh in range(GH)
    ]
    both = [
        merge(n2[hh], t2[hh], num3[hh], jnp.where(((row64 >> 2) & 3) == digits[hh][2], soft[hh][1], LOW))
        for hh in range(GH)
    ]
    for hh in range(GH):
        _, _, b2, b3 = bits(sm[x, hh], (16, 128))
        part = jnp.concatenate(
            [pick([nm[hh, j * 64 + i * 16 : j * 64 + (i + 1) * 16, :] for i in range(4)], b2, b3) for j in range(NX)],
            axis=0,
        )
        _, _, b2, b3 = bits(sm[x, hh], (16, 1))
        part_top = jnp.concatenate(
            [pick([tm[hh, j * 64 + i * 16 : j * 64 + (i + 1) * 16, :] for i in range(4)], b2, b3) for j in range(NX)],
            axis=0,
        )
        num, _ = merge(part, part_top, *both[hh])
        value = quotient(num, hh % 2 == 0).astype(BF)
        place = jnp.zeros((16, 128), jnp.int32) + (digits[hh][0] * 4 + digits[hh][1])
        side = [low16, jnp.logical_not(low16), low16][hh]
        lanes = slice(hh // 2 * 128, (hh // 2 + 1) * 128)
        for i in range(16):
            mask = (place == i) & side
            rows = slice(i * 16, (i + 1) * 16)
            for j in range(NX):
                outp[j, rows, lanes] = jnp.where(mask, value[j * 16 : (j + 1) * 16], outp[j, rows, lanes])
    for j in range(NX):
        final = lax.dot_general(
            outp[j], perm[...], (((0,), (0,)), ((), ())), preferred_element_type=F32
        )
        out[:, j * ROWS : (j + 1) * ROWS] = final[: GH * HD].astype(BF)

    for copy in (*r_copies[2], f2_copy, f3_copy):
        copy.wait_send()


def per_device(qkv, offsets):
    dma = pltpu.SemaphoreType.DMA
    turned = pl.pallas_call(
        kernel,
        out_shape=jax.ShapeDtypeStruct((GH * HD, NX * ROWS), BF),
        in_specs=[pl.BlockSpec(memory_space=pltpu.HBM), pl.BlockSpec(memory_space=pltpu.HBM)],
        out_specs=pl.BlockSpec(memory_space=pltpu.VMEM),
        scratch_shapes=[
            pltpu.VMEM((3, ROWS, 768), BF),
            pltpu.VMEM((ROWS, ROWS), BF),
            pltpu.VMEM((NX, GH, 128, 128), BF),
            pltpu.VMEM((NX, GH, ROWS, 128), BF),
            pltpu.VMEM((NX, GH, ROWS, 128), BF),
            pltpu.VMEM((GH, NX, 128, 128), BF),
            pltpu.VMEM((GH, NX, ROWS, 128), BF),
            pltpu.VMEM((GH, NX, ROWS, 128), BF),
            pltpu.VMEM((GH, NX, 64, 128), BF),
            pltpu.VMEM((GH, NX, 16, 128), BF),
            pltpu.VMEM((2 * N2, GH, NX, 16, 128), BF),
            pltpu.VMEM((GH, 16, 128), BF),
            pltpu.VMEM((2 * N3, GH, 16, 128), BF),
            pltpu.SMEM((GH,), jnp.int32),
            pltpu.SMEM((NX, 128), jnp.int32),
            pltpu.VMEM((GH, NX, ROWS, 128), F32),
            pltpu.VMEM((GH, NX, ROWS, 1), F32),
            pltpu.VMEM((GH, ROWS, 128), F32),
            pltpu.VMEM((GH, ROWS, 1), F32),
            pltpu.VMEM((GH, ROWS, 128), F32),
            pltpu.VMEM((GH, ROWS, 1), F32),
            pltpu.VMEM((GH, 64, 512), F32),
            pltpu.VMEM((GH, 512, 128), BF),
            pltpu.VMEM((GH, 64, 128), F32),
            pltpu.VMEM((GH, 64, 1), F32),
            pltpu.VMEM((NX, ROWS, 256), BF),
            dma((3,)), dma((8,)), dma((2, 3)), dma((3,)), dma((GH, 3)), dma((GH, 3)), dma((3,)), dma((3,)),
            dma((3,)), dma((3,)), dma((GH, 3)), dma((GH, 3)), dma, dma, dma((N2,)), dma((N2,)), dma((N3,)), dma((N3,)),
            dma((2,)), dma((2,)),
            pltpu.SemaphoreType.REGULAR,
        ],
        compiler_params=pltpu.CompilerParams(
            collective_id=0, has_side_effects=True, vmem_limit_bytes=40 * 2**20
        ),
        cost_estimate=pl.CostEstimate(flops=10**9, bytes_accessed=2 * 10**6, transcendentals=2 * 10**6),
    )(pltpu.with_memory_space_constraint(qkv, pltpu.HBM), pltpu.with_memory_space_constraint(offsets, pltpu.HBM))
    return turned.T


def solution(mesh):
    return jax.shard_map(
        per_device,
        mesh=mesh,
        in_specs=(P(None, ("seq", "head"), None), P("head")),
        out_specs=P("seq", "head"),
        check_vma=False,
    )
```
